32 devices in a mesh: dp: 2 (over x), blk: 4 (over z), mp: 4 (over y, core).
Axes of the slice: x: 2, y: 2, z: 4, core: 2. Of those that a mesh axis runs over, the one named last changes fastest.
Arguments:
- inputs: bfloat16 [8, 512, 2048], P('dp', 'blk'), may hold values from -6 to 6
- lengths: int32 [8], P('dp'), may hold values from 288 to 512, as said below
- w_qkv: bfloat16 [2048, 3, 2048], P(None, None, 'mp'), may hold values from -0.125 to 0.125
- b_qv: bfloat16 [2, 2048], P(None, 'mp'), may hold values from -3 to 3
- w_out: bfloat16 [2048, 2048], P(None, 'mp'), may hold values from -0.5 to 0.5
- out_biases: bfloat16 [2, 2048], replicated, may hold values from -2 to 2
- ln_gains: bfloat16 [2, 2048], replicated, may hold values from 0.25 to 1.75
- ln_shifts: bfloat16 [2, 2048], replicated, may hold values from -2 to 2
- w_up: bfloat16 [2048, 8192], P(None, 'mp'), may hold values from -0.125 to 0.125
- b_up: bfloat16 [8192], P('mp'), may hold values from -3 to 3
- w_down: bfloat16 [2048, 8192], P(None, 'mp'), may hold values from -0.0625 to 0.0625
- cotangent: bfloat16 [8, 512, 2048], P('dp', 'blk'), may hold values from -6 to 6
Outputs:
- output: bfloat16 [8, 512, 2048], P('dp', 'blk')
- input_grad: float32 [8, 512, 2048], P('dp', 'blk')
- grad_qkv: float32 [2048, 3, 2048], P(('dp', 'blk'), None, 'mp')
- grad_qv_bias: float32 [2, 2048], P(None, 'mp')
- grad_out: float32 [2048, 2048], P(('dp', 'blk'), 'mp')
- grad_out_biases: float32 [2, 2048], replicated
- grad_gains: float32 [2, 2048], replicated
- grad_shifts: float32 [2, 2048], replicated
- grad_up: float32 [2048, 8192], P(('dp', 'blk'), 'mp')
- grad_up_bias: float32 [8192], P('mp')
- grad_down: float32 [2048, 8192], P(('dp', 'blk'), 'mp')
The draws below stay inside these ranges and needn't reach their ends.
Inputs may be any that keep to these rules, and one draw needn't show every extreme that they name: `lengths`: each length is 256 plus a positive multiple of 32; in each aligned block of 4 items one item, drawn from the seed, has length 512.
All inputs are finite; a program needn't handle non-finite values.
Results may differ from the reference program's by a relative error of at most 0.019.
Values may be sent and summed in bfloat16 or wider, within the bound.
No kernel may reach another device: no remote copies, remote signals or barrier semaphores. Data moves between devices by JAX's collectives and lax.ppermute only.
A program may use at most 192 MiB of HBM per device.

```python
import jax
import jax.numpy as jnp
from jax import lax

D = 2048
HEADS = 16
DH = 128
FF = 8192
GOAL = 256
STEP = 32
STEPS = 8
ITEMS_DEV = 4
LEN = 512
HD = 2048
ITEMS = 8


def draw_lengths(key, part):
    key = jax.random.fold_in(key, 7)
    key_steps, key_full = jax.random.split(key)
    steps = jax.random.randint(key_steps, (ITEMS,), 1, STEPS + 1)
    chosen = jax.random.randint(key_full, (ITEMS // ITEMS_DEV,), 0, ITEMS_DEV)
    index = jnp.arange(ITEMS, dtype=jnp.int32)
    slot = index % ITEMS_DEV
    owner = jnp.repeat(chosen, ITEMS_DEV)
    steps = jnp.where(slot == owner, STEPS, steps)
    return (GOAL + STEP * steps).astype(jnp.int32)


def with_spikes(values, own_key, source, target, blocks, factor):
    owner, partner = [(jnp.arange(values.shape[axis_at]) // (values.shape[axis_at] // blocks)).reshape([-1 if axis == axis_at else 1 for axis in range(values.ndim)]) for axis_at in (source, target)]
    chosen = jax.random.permutation(own_key, blocks)[partner]
    strong = (owner == chosen) | (owner == (partner + blocks // 2) % blocks)
    return jnp.where(strong, factor * values, values)


def block_levels(own_key, extent, cuts, low, top_value):
    level, own = 1.0, jax.random.fold_in(own_key, 6)
    for axis_at, parts in cuts:
        heights = jnp.exp(jax.random.uniform(jax.random.fold_in(own, axis_at), (parts,), jnp.float32, low / len(cuts), top_value / len(cuts)))
        level = level * jnp.repeat(heights, extent[axis_at] // parts).reshape([-1 if axis == axis_at else 1 for axis in range(len(extent))])
    return level


def centred(own_key, dims, spread, reach, pieces=(), kind=jnp.bfloat16):
    entries = jax.random.normal(own_key, dims, jnp.float32) * spread
    if len(pieces) > 0:
        entries = block_levels(own_key, dims, pieces, -0.22, 0.18) * entries
    return jnp.clip(entries, min=-reach, max=reach).astype(kind)


def heavy_noise(key, extent, scale, most, shards, heavy, kind=jnp.bfloat16):
    values = scale * jax.random.normal(key, extent, jnp.float32)
    if shards:
        values = values * block_levels(key, extent, shards, -0.22, 0.18)
    return jnp.clip(with_spikes(values, jax.random.fold_in(key, 3), *heavy), -most, most).astype(kind)


def setup_inputs(seed: int = 0) -> dict:
    splits = jax.random.split(jax.random.key(seed), 13)
    inputs = centred(splits[0], (ITEMS, LEN, D), 1.0, 6.0, ((0, 2), (1, 4)))
    lengths = draw_lengths(jax.random.fold_in(splits[12], 71), 0)
    w_qkv = centred(splits[2], (D, 3, HD), D ** -0.5, 0.125, ((2, 4),))
    b_qv = centred(splits[3], (2, HD), 0.5, 3.0, ((1, 4),))
    w_out = centred(splits[4], (D, HD), (HD // 16) ** -0.5, 0.5, ((1, 4),))
    out_biases = centred(splits[5], (2, D), 0.3, 2.0)
    ln_gains = jnp.clip(1.0 + 0.15 * jax.random.normal(splits[6], (2, D), jnp.float32), 0.25, 1.75).astype(jnp.bfloat16)
    ln_shifts = centred(splits[7], (2, D), 0.3, 2.0)
    w_up = centred(splits[8], (D, FF), D ** -0.5, 0.125, ((1, 4),))
    b_up = centred(splits[9], (FF,), 0.5, 3.0, ((0, 4),))
    w_down = centred(splits[10], (D, FF), FF ** -0.5, 0.0625, ((1, 4),))
    cotangent = heavy_noise(splits[11], (ITEMS, LEN, D), 1.0, 6.0, ((0, 2), (1, 4)), (0, 2, 2, 2.0))
    return {"inputs": inputs, "lengths": lengths, "w_qkv": w_qkv, "b_qv": b_qv, "w_out": w_out, "out_biases": out_biases, "ln_gains": ln_gains, "ln_shifts": ln_shifts, "w_up": w_up, "b_up": b_up, "w_down": w_down, "cotangent": cotangent}


@jax.custom_vjp
def low(v):
    return lax.optimization_barrier(v.astype(jnp.bfloat16)).astype(jnp.float32)

@jax.custom_vjp
def low_back(v):
    return v

def low_keep(v):
    return (low(v), None)

def low_pass(kept, grad):
    return (grad,)

def back_keep(v):
    return (v, None)

def back_low(kept, grad):
    return (low(grad),)
low.defvjp(low_keep, low_pass)
low_back.defvjp(back_keep, back_low)
highest = lax.Precision.HIGHEST

def layer_norm(values, gain, shift):
    centered = values - lax.optimization_barrier(jnp.mean(values, axis=-1, keepdims=True))
    variance = lax.optimization_barrier(jnp.mean(centered * centered, axis=-1, keepdims=True))
    return centered * lax.rsqrt(variance + 1e-05) * gain + shift

def block_forward(params, rows, lengths_group):
    w_qkv, b_qv, w_out, out_biases, ln_gains, ln_shifts, w_up, b_up, w_down = params
    group = rows.shape[0]
    normed = low(layer_norm(rows, ln_gains[0], ln_shifts[0]))
    projected = jnp.einsum('gpd,dth->tgph', normed, w_qkv, precision=highest)
    queries = low(low_back(projected[0] + b_qv[0])).reshape(group, LEN, HEADS, DH)
    keys_all = low(low_back(projected[1])).reshape(group, LEN, HEADS, DH)
    values_all = low(low_back(projected[2] + b_qv[1])).reshape(group, LEN, HEADS, DH)
    raw = low_back(jnp.einsum('gind,gjnd->gnij', queries, keys_all, precision=highest))
    scaled = raw * DH ** (-0.5)
    positions = jnp.arange(LEN, dtype=jnp.int32)
    causal = positions[None, None, None, :] <= positions[None, None, :, None]
    inside = positions[None, None, None, :] < lengths_group.astype(jnp.int32)[:, None, None, None]
    scores = jnp.where(causal & inside, scaled, -1e+30)
    probs = jax.nn.softmax(scores, axis=-1)
    mixed = jnp.einsum('gnij,gjnd->gind', low(probs), values_all, precision=highest)
    mixed = low(low_back(mixed.reshape(group, LEN, HD)))
    attn = low_back(jnp.einsum('gph,dh->gpd', mixed, w_out, precision=highest) + out_biases[0])
    resid = rows + attn
    normed_two = low(layer_norm(resid, ln_gains[1], ln_shifts[1]))
    upper = low_back(jnp.einsum('gpd,df->gpf', normed_two, w_up, precision=highest) + b_up)
    gelu_vals = low(jax.nn.gelu(upper, approximate=False))
    down = low_back(jnp.einsum('gpf,df->gpd', gelu_vals, w_down, precision=highest) + out_biases[1])
    return resid + down

def reference(inputs, lengths, w_qkv, b_qv, w_out, out_biases, ln_gains, ln_shifts, w_up, b_up, w_down, cotangent):
    params = tuple((arr.astype(jnp.float32) for arr in (w_qkv, b_qv, w_out, out_biases, ln_gains, ln_shifts, w_up, b_up, w_down)))
    groups = ITEMS // ITEMS_DEV
    stacked = inputs.astype(jnp.float32).reshape(groups, ITEMS_DEV, LEN, D)
    length_groups = lengths.astype(jnp.int32).reshape(groups, ITEMS_DEV)

    def whole(values, weights):
        step_fn = jax.checkpoint(block_forward)
        return lax.map(lambda pair: step_fn(weights, pair[0], pair[1]), (values, length_groups))
    result, pullback = jax.vjp(whole, stacked, params)
    positions = jnp.arange(LEN, dtype=jnp.int32)
    valid = (positions[None, :] < lengths.astype(jnp.int32)[:, None]).astype(jnp.float32)
    grad_y = (cotangent.astype(jnp.float32) * valid[:, :, None]).reshape(groups, ITEMS_DEV, LEN, D)
    grad_inputs, grad_params = pullback(grad_y)
    output = result.reshape(ITEMS, LEN, D).astype(jnp.bfloat16)
    input_grad = grad_inputs.reshape(ITEMS, LEN, D)
    return (output, input_grad, grad_params[0], grad_params[1], grad_params[2], grad_params[3], grad_params[4], grad_params[5], grad_params[6], grad_params[7], grad_params[8])
```

```python
import jax
import jax.numpy as jnp
from jax import lax
from jax.sharding import PartitionSpec as P

DH = 128
LOW = jnp.bfloat16
FULL = jnp.float32


def flip(size, bit):
    return [(i, i ^ bit) for i in range(size)]


def shift(size, step):
    return [(i, (i + step) % size) for i in range(size)]


def normalize(values):
    centered = values - jnp.mean(values, axis=-1, keepdims=True)
    variance = jnp.mean(centered * centered, axis=-1, keepdims=True)
    inverse = lax.rsqrt(variance + 1e-05)
    return centered * inverse, inverse


def norm_back(grad_norm, unit, inverse, gain):
    scaled = grad_norm * gain
    first = jnp.mean(scaled, axis=-1, keepdims=True)
    second = jnp.mean(scaled * unit, axis=-1, keepdims=True)
    return inverse * (scaled - first - unit * second)


def exact_gelu(values):
    return jax.nn.gelu(values, approximate=False)


def dot(left, right, dims):
    return lax.dot_general(left, right, (dims, ((), ())), preferred_element_type=FULL)


def on_device(
    dp,
    blk,
    mp,
    inputs,
    lengths,
    w_qkv,
    b_qv,
    w_out,
    out_biases,
    ln_gains,
    ln_shifts,
    w_up,
    b_up,
    w_down,
    cotangent,
):
    items, block_len, d_model = inputs.shape
    width = w_qkv.shape[2]
    heads = width // DH
    scale = DH ** (-0.5)
    sub = block_len // mp
    own_rows = blk * sub
    rows = own_rows * mp
    chunk = d_model // (dp * blk)
    x, z, me = lax.axis_index("dp"), lax.axis_index("blk"), lax.axis_index("mp")
    gains = ln_gains.astype(FULL)
    shifts = ln_shifts.astype(FULL)
    biases = out_biases.astype(FULL)

    def to_items(array):
        mine = lax.dynamic_slice_in_dim(array, me * sub, sub, axis=1)
        parts = [lax.dynamic_index_in_dim(mine, z, 0, keepdims=False)]
        for s in range(1, blk):
            piece = lax.dynamic_index_in_dim(mine, lax.rem(z + s, blk), 0, keepdims=False)
            parts.append(lax.ppermute(piece, "blk", shift(blk, s)))
        return jnp.concatenate(parts, axis=0)

    def gather_mp(own):
        half = jnp.concatenate([own, lax.ppermute(own, "mp", flip(mp, 2))], axis=0)
        return jnp.concatenate([half, lax.ppermute(half, "mp", flip(mp, 1))], axis=0)

    def scatter_mp(keep, send):
        keep = keep + lax.ppermute(send.astype(LOW), "mp", flip(mp, 1)).astype(FULL)
        got = lax.ppermute(keep[own_rows:].astype(LOW), "mp", flip(mp, 2))
        return keep[:own_rows] + got.astype(FULL)

    def from_items(own):
        parts = [own[:sub]]
        for s in range(1, blk):
            parts.append(lax.ppermute(own[s * sub : (s + 1) * sub], "blk", shift(blk, -s)))
        whole = gather_mp(jnp.concatenate(parts, axis=0)).reshape(mp, blk, sub, d_model)
        order = [0, 2, 1, 3]
        result = jnp.zeros((items, mp, sub, d_model), own.dtype)
        for at, j in enumerate(order):
            for s in range(blk):
                result = lax.dynamic_update_slice(
                    result, whole[at, s][None, None], (lax.rem(z + s, blk), me ^ j, 0, 0)
                )
        return result.reshape(items, block_len, d_model)

    in_block = jnp.arange(sub, dtype=jnp.int32)
    block_of = lax.rem(z - jnp.arange(blk, dtype=jnp.int32) + blk, blk)

    def positions_of(q):
        return (block_of[:, None] * block_len + q * sub + in_block[None, :]).reshape(-1)

    pos_own = positions_of(me)
    pos = jnp.concatenate([positions_of(me ^ j) for j in (0, 2, 1, 3)])
    length = lax.dynamic_index_in_dim(lengths, z, 0, keepdims=False)

    def ring_columns(array, parts):
        pieces = []
        for k in range(blk):
            at = lax.rem(z + k, blk)
            for part in parts:
                pieces.append(
                    lax.dynamic_slice_in_dim(array, (part * blk + at) * chunk, chunk, axis=1)
                )
        return jnp.concatenate(pieces, axis=1)

    def ring_scatter(partial):
        far = partial(2).astype(LOW)
        cut = far.shape[1] // 2
        from_left = lax.ppermute(far[:, :cut], "blk", shift(blk, 1))
        from_right = lax.ppermute(far[:, cut:], "blk", shift(blk, -1))
        right = partial(1)
        left = partial(3)
        right = jnp.concatenate([right[:, :cut] + from_left.astype(FULL), right[:, cut:]], axis=1)
        left = jnp.concatenate([left[:, :cut], left[:, cut:] + from_right.astype(FULL)], axis=1)
        from_left = lax.ppermute(right.astype(LOW), "blk", shift(blk, 1))
        from_right = lax.ppermute(left.astype(LOW), "blk", shift(blk, -1))
        return partial(0) + from_left.astype(FULL) + from_right.astype(FULL)

    other = [1 - x]

    def swap_dp(array):
        return lax.ppermute(array, "dp", flip(dp, 1))

    def all_columns(d_side):
        return ring_columns(d_side, list(range(dp)))

    def grad_all(d_cols, n_side):
        size = dp * chunk

        def partial(k):
            return dot(d_cols[:, k * size : (k + 1) * size], n_side, ((0,), (0,)))

        summed = ring_scatter(partial)
        if dp == 2:
            mine = lax.dynamic_slice_in_dim(summed, x * chunk, chunk, axis=0)
            theirs = lax.dynamic_slice_in_dim(summed, (1 - x) * chunk, chunk, axis=0)
            return mine + swap_dp(theirs.astype(LOW)).astype(FULL)
        return lax.psum_scatter(
            summed.astype(LOW), "dp", scatter_dimension=0, tiled=True
        ).astype(FULL)

    def grad_half(d_own, d_other, n_own):
        n_other = swap_dp(n_own)

        def partial(k):
            at = slice(k * chunk, (k + 1) * chunk)
            return dot(d_own[:, at], n_own, ((0,), (0,))) + dot(
                d_other[:, at], n_other, ((0,), (0,))
            )

        return ring_scatter(partial)

    def other_columns(own):
        return gather_mp(swap_dp(ring_columns(own, other)))

    def weight_grad(own, full, n_side):
        if dp == 2:
            return grad_half(ring_columns(full, [x]), other_columns(own), n_side)
        return grad_all(all_columns(full), n_side)

    x_own = to_items(inputs).astype(FULL)
    unit_one, inverse_one = normalize(x_own)
    act_one_own = (unit_one * gains[0] + shifts[0]).astype(LOW)
    act_one = gather_mp(act_one_own)
    qv_bias = b_qv.astype(FULL)

    def project(t):
        return dot(act_one, w_qkv[:, t], ((1,), (0,)))

    def by_head(array):
        return array.reshape(rows, heads, DH).transpose(1, 0, 2)

    queries = by_head((project(0) + qv_bias[0]).astype(LOW))
    keys = by_head(project(1).astype(LOW))
    values = by_head((project(2) + qv_bias[1]).astype(LOW))
    allowed = (pos[None, :] <= pos[:, None]) & (pos[None, :] < length)
    scores = jnp.einsum("nid,njd->nij", queries, keys, preferred_element_type=FULL)
    scores = jnp.where(allowed[None], scores * scale, -1e30)
    peak = jnp.max(scores, axis=-1, keepdims=True)
    expo = jnp.exp(scores - peak)
    probs = expo / jnp.sum(expo, axis=-1, keepdims=True)
    mixed = jnp.einsum("nij,njd->ind", probs.astype(LOW), values, preferred_element_type=FULL)
    mixed = mixed.reshape(rows, width).astype(LOW)
    half = rows // 2

    def halves(left, right, dims):
        return dot(left[:half], right, dims), dot(left[half:], right, dims)

    attn = scatter_mp(*halves(mixed, w_out, ((1,), (1,)))) + biases[0]
    resid = x_own + attn
    unit_two, inverse_two = normalize(resid)
    act_two_own = (unit_two * gains[1] + shifts[1]).astype(LOW)
    act_two = gather_mp(act_two_own)

    dy_own = to_items(cotangent).astype(FULL) * (pos_own < length).astype(FULL)[:, None]
    dy_own_low = dy_own.astype(LOW)
    dy = gather_mp(dy_own_low)

    upper = dot(act_two, w_up, ((1,), (0,))) + b_up.astype(FULL)
    gelu_vals, gelu_back = jax.vjp(exact_gelu, upper)
    gel = gelu_vals.astype(LOW)
    dup = gelu_back(dot(dy, w_down, ((1,), (0,))))[0].astype(LOW)
    da2 = scatter_mp(*halves(dup, w_up, ((1,), (1,))))
    dh = dy_own + norm_back(da2, unit_two, inverse_two, gains[1])
    dattn_own = dh.astype(LOW)
    dattn = gather_mp(dattn_own)
    dmixed = by_head(dot(dattn, w_out, ((1,), (0,))).astype(LOW))

    down = scatter_mp(*halves(gel, w_down, ((1,), (1,)))) + biases[1]
    output = from_items((resid + down).astype(LOW))

    dv = jnp.einsum("nij,nid->jnd", probs.astype(LOW), dmixed, preferred_element_type=FULL)
    dprobs = jnp.einsum("nid,njd->nij", dmixed, values, preferred_element_type=FULL)
    row_terms = jnp.sum(probs * dprobs, axis=-1, keepdims=True)
    dscores = (probs * (dprobs - row_terms) * scale).astype(LOW)
    dq = jnp.einsum("nij,njd->ind", dscores, keys, preferred_element_type=FULL)
    dk = jnp.einsum("nij,nid->jnd", dscores, queries, preferred_element_type=FULL)
    dqkv = [part.astype(LOW).reshape(rows, width) for part in (dq, dk, dv)]

    def da1_part(at):
        return sum(dot(dqkv[t][at], w_qkv[:, t], ((1,), (1,))) for t in range(3))

    da1 = scatter_mp(da1_part(slice(0, half)), da1_part(slice(half, rows)))
    input_grad = dh + norm_back(da1, unit_one, inverse_one, gains[0])
    input_grad = from_items(input_grad.astype(LOW)).astype(FULL)

    grad_down = weight_grad(dy_own_low, dy, gel)
    grad_up = weight_grad(act_two_own, act_two, dup)
    grad_out = grad_all(all_columns(dattn), mixed)
    grad_qkv = weight_grad(act_one_own, act_one, jnp.concatenate(dqkv, axis=1))
    grad_qkv = grad_qkv.reshape(chunk, 3, width)

    def sum_over(array, axis, size):
        bit = 1
        while bit < size:
            array = array + lax.ppermute(array, axis, flip(size, bit))
            bit *= 2
        return array

    def column_sum(array):
        return jnp.sum(array.astype(FULL), axis=0)

    def sum_groups(array):
        return sum_over(sum_over(array, "blk", blk), "dp", dp)

    first = jnp.concatenate(
        [column_sum(da2 * unit_two), column_sum(da2), column_sum(dattn_own), column_sum(dy_own)]
    )
    first = jnp.concatenate([sum_over(first, "mp", mp), column_sum(dup)])
    first = sum_groups(first)
    last = jnp.concatenate([column_sum(da1 * unit_one), column_sum(da1)])
    last = jnp.concatenate([sum_over(last, "mp", mp), column_sum(dqkv[0]), column_sum(dqkv[2])])
    last = sum_groups(last)
    gain_two, shift_two, attn_bias, down_bias = [
        first[i * d_model : (i + 1) * d_model] for i in range(4)
    ]
    grad_up_bias = first[4 * d_model :]
    gain_one, shift_one = last[:d_model], last[d_model : 2 * d_model]
    grad_qv_bias = last[2 * d_model :].reshape(2, width)
    return (
        output,
        input_grad,
        grad_qkv,
        grad_qv_bias,
        grad_out,
        jnp.stack([attn_bias, down_bias]),
        jnp.stack([gain_one, gain_two]),
        jnp.stack([shift_one, shift_two]),
        grad_up,
        grad_up_bias,
        grad_down,
    )


def solution(mesh):
    sizes = [mesh.shape[name] for name in ("dp", "blk", "mp")]
    in_specs = (
        P("dp", "blk", None),
        P("dp"),
        P(None, None, "mp"),
        P(None, "mp"),
        P(None, "mp"),
        P(),
        P(),
        P(),
        P(None, "mp"),
        P("mp"),
        P(None, "mp"),
        P("dp", "blk", None),
    )
    out_specs = (
        P("dp", "blk", None),
        P("dp", "blk", None),
        P(("dp", "blk"), None, "mp"),
        P(None, "mp"),
        P(("dp", "blk"), "mp"),
        P(),
        P(),
        P(),
        P(("dp", "blk"), "mp"),
        P("mp"),
        P(("dp", "blk"), "mp"),
    )

    def step(*arrays):
        return on_device(*sizes, *arrays)

    return jax.shard_map(
        step, mesh=mesh, in_specs=in_specs, out_specs=out_specs, check_vma=False
    )
```

```python
import functools

import jax
import jax.numpy as jnp
from jax import lax
from jax.experimental import pallas as pl
from jax.experimental.pallas import tpu as pltpu
from jax.sharding import PartitionSpec as P

DH = 128
LOW = jnp.bfloat16
FULL = jnp.float32
TILE = 512


def flip(size, bit):
    return [(i, i ^ bit) for i in range(size)]


def shift(size, step):
    return [(i, (i + step) % size) for i in range(size)]


def after(value, *others):
    return lax.optimization_barrier((value, *others))[0]


class Order:
    def __init__(self):
        self.last = None

    def run(self, function, first, *others, needs=()):
        waits = list(needs) + ([] if self.last is None else [self.last])
        if waits:
            first = after(first, *waits)
        results = function(first, *others)
        self.last = results[-1] if isinstance(results, (list, tuple)) else results
        return results


def dot(left, right, dims):
    return lax.dot_general(left, right, (dims, ((), ())), preferred_element_type=FULL)


COLS = ((1,), (0,))
BOTH = ((1,), (1,))
ROWS = ((0,), (0,))


def shape_of(dims, kind):
    return jax.ShapeDtypeStruct(dims, kind)


def whole(dims):
    return pl.BlockSpec(dims, lambda *_: (0,) * len(dims))


def params(megabytes):
    return pltpu.CompilerParams(vmem_limit_bytes=megabytes << 20)


def cost(microseconds):
    flops = int(microseconds * 0.2 * 1153.5e6)
    return pl.CostEstimate(flops=flops, bytes_accessed=1, transcendentals=0)


def stack_rows(target, pieces):
    at = 0
    for piece in pieces:
        target[at : at + piece.shape[0], :] = piece[...]
        at += piece.shape[0]


def normalize(values):
    centered = values - jnp.mean(values, axis=-1, keepdims=True)
    variance = jnp.mean(centered * centered, axis=-1, keepdims=True)
    inverse = lax.rsqrt(variance + 1e-05)
    return centered * inverse, inverse


def norm_back(grad_norm, unit, inverse, gain):
    scaled = grad_norm * gain
    first = jnp.mean(scaled, axis=-1, keepdims=True)
    second = jnp.mean(scaled * unit, axis=-1, keepdims=True)
    return inverse * (scaled - first - unit * second)


def enter_kernel(count, gain, bias, *refs):
    pieces, (x_out, act_out) = refs[:count], refs[count:]
    stack_rows(x_out, pieces)
    unit, _ = normalize(x_out[...].astype(FULL))
    act_out[...] = (unit * gain[...].astype(FULL) + bias[...].astype(FULL)).astype(LOW)


def enter(gain, bias, pieces):
    rows, d_model = sum(p.shape[0] for p in pieces), pieces[0].shape[1]
    return pl.pallas_call(
        functools.partial(enter_kernel, len(pieces)),
        out_shape=[shape_of((rows, d_model), LOW)] * 2,
        compiler_params=params(16),
        cost_estimate=cost(2),
    )(gain, bias, *pieces)


def attention_kernel(scale, own, near, far, last, w_qkv, b_qkv, w_out, pos_row, pos_col, length, qkv_out, probs_out, mixed_out, keep_out, send_out, fold_out, act, bias, total):
    step = pl.program_id(0)
    half = act.shape[0] // 2

    @pl.when(step == 0)
    def _():
        stack_rows(act, (own, near, far, last))
        allowed = (pos_row[...] <= pos_col[...]) & (pos_row[...] < length[0])
        bias[...] = jnp.where(allowed, 0.0, -1e30)
        total[...] = jnp.zeros_like(total)

    for t in range(3):
        qkv_out[t] = (dot(act[...], w_qkv[t], COLS) + b_qkv[t][None]).astype(LOW)
    for h in range(w_out.shape[1] // DH):
        at = slice(h * DH, (h + 1) * DH)
        scores = dot(qkv_out[0, :, at], qkv_out[1, :, at], BOTH) * scale + bias[...]
        expo = jnp.exp(scores - jnp.max(scores, axis=-1, keepdims=True))
        probs = expo * (1.0 / jnp.sum(expo, axis=-1, keepdims=True))
        probs_out[h] = probs
        mixed_out[:, at] = dot(probs.astype(LOW), qkv_out[2, :, at], COLS).astype(LOW)
    total[...] += dot(mixed_out[...], w_out[...], BOTH)

    @pl.when(step == pl.num_programs(0) - 1)
    def _():
        keep_out[...] = total[:half]
        send_out[...] = total[half : half + half // 2].astype(LOW)
        fold_out[...] = total[half + half // 2 :].astype(LOW)


def attention(own, near, far, last, w_qkv, b_qkv, w_out, pos, length, group=2):
    d_model, width = w_out.shape
    rows = 4 * own.shape[0]
    cols = group * DH
    heads = width // DH
    return pl.pallas_call(
        functools.partial(attention_kernel, DH**-0.5),
        grid=(width // cols,),
        in_specs=[
            *[whole(own.shape)] * 4,
            pl.BlockSpec((3, d_model, cols), lambda i: (0, 0, i)),
            pl.BlockSpec((3, cols), lambda i: (0, i)),
            pl.BlockSpec((d_model, cols), lambda i: (0, i)),
            whole((1, rows)),
            whole((rows, 1)),
            pl.BlockSpec(memory_space=pltpu.SMEM),
        ],
        out_specs=[
            pl.BlockSpec((3, rows, cols), lambda i: (0, 0, i)),
            pl.BlockSpec((group, rows, rows), lambda i: (i, 0, 0)),
            pl.BlockSpec((rows, cols), lambda i: (0, i)),
            whole((rows // 2, d_model)),
            whole((rows // 4, d_model)),
            whole((rows // 4, d_model)),
        ],
        out_shape=[
            shape_of((3, rows, width), LOW),
            shape_of((heads, rows, rows), FULL),
            shape_of((rows, width), LOW),
            shape_of((rows // 2, d_model), FULL),
            shape_of((rows // 4, d_model), LOW),
            shape_of((rows // 4, d_model), LOW),
        ],
        scratch_shapes=[
            pltpu.VMEM((rows, d_model), LOW),
            pltpu.VMEM((rows, rows), FULL),
            pltpu.VMEM((rows, d_model), FULL),
        ],
        compiler_params=params(48),
        cost_estimate=cost(14),
    )(own, near, far, last, w_qkv, b_qkv, w_out, pos[None, :], pos[:, None], length)


def fold_kernel(got, keep, out):
    out[...] = (keep[...] + got[...].astype(FULL)).astype(LOW)


def fold(got, keep):
    rows, d_model = got.shape
    lower = pl.BlockSpec((rows, d_model), lambda i: (1, 0))
    return pl.pallas_call(
        fold_kernel,
        grid=(1,),
        in_specs=[whole(got.shape), lower],
        out_specs=whole((rows, d_model)),
        out_shape=shape_of((rows, d_model), LOW),
        compiler_params=params(16),
        cost_estimate=cost(1),
    )(got, keep)


def output_kernel(last, keep, got, resid, biases, out):
    down = keep[...] + got[...].astype(FULL) + last[...].astype(FULL)
    out[...] = (resid[...] + down + biases[1:].astype(FULL)).astype(LOW)


def output_of(last, keep, got, resid, biases):
    dims = resid.shape
    return pl.pallas_call(
        output_kernel,
        grid=(1,),
        in_specs=[whole(dims)] * 4 + [whole(biases.shape)],
        out_specs=whole(dims),
        out_shape=shape_of(dims, LOW),
        compiler_params=params(16),
        cost_estimate=cost(1.5),
    )(last, keep, got, resid, biases)


def middle_kernel(x_own, keep, got, last, biases, gain, bias, resid_out, act_out):
    attn = keep[...] + got[...].astype(FULL) + last[...].astype(FULL) + biases[:1].astype(FULL)
    resid = x_own[...].astype(FULL) + attn
    resid_out[...] = resid
    unit, _ = normalize(resid)
    act_out[...] = (unit * gain[...].astype(FULL) + bias[...].astype(FULL)).astype(LOW)


def middle(x_own, keep, got, last, biases, gain, bias):
    dims = x_own.shape
    return pl.pallas_call(
        middle_kernel,
        grid=(1,),
        in_specs=[whole(dims)] * 4 + [whole(biases.shape), whole(gain.shape), whole(bias.shape)],
        out_specs=[whole(dims)] * 2,
        out_shape=[shape_of(dims, FULL), shape_of(dims, LOW)],
        compiler_params=params(24),
        cost_estimate=cost(2),
    )(x_own, keep, got, last, biases, gain, bias)


def feed_kernel(own, near, far, last, dy_own, dy_near, dy_far, dy_last, w_up, b_up, w_down, gel_out, dup_out, sum_out, keep_out, send_out, fold_out, act, dy, total):
    step = pl.program_id(0)
    half = act.shape[0] // 2

    @pl.when(step == 0)
    def _():
        stack_rows(act, (own, near, far, last))
        stack_rows(dy, (dy_own, dy_near, dy_far, dy_last))
        total[...] = jnp.zeros_like(total)

    upper = dot(act[...], w_up[...], COLS) + b_up[...].astype(FULL)
    dgel = dot(dy[...], w_down[...], COLS)
    phi = 0.5 + 0.5 * lax.erf(upper * (0.5**0.5))
    gel_out[0] = (upper * phi).astype(LOW)
    slope = phi + upper * jnp.exp(-0.5 * upper * upper) * 0.3989422804014327
    dup = (dgel * slope).astype(LOW)
    dup_out[0] = dup
    sum_out[...] = jnp.sum(dup.astype(FULL), axis=0, keepdims=True)
    total[...] += dot(dup, w_up[...], BOTH)

    @pl.when(step == pl.num_programs(0) - 1)
    def _():
        keep_out[...] = total[:half]
        send_out[...] = total[half : half + half // 2].astype(LOW)
        fold_out[...] = total[half + half // 2 :].astype(LOW)


def feed(own, near, far, last, dy, w_up, b_up, w_down):
    d_model, units = w_up.shape
    rows = 4 * own.shape[0]
    steps = units // TILE
    return pl.pallas_call(
        feed_kernel,
        grid=(steps,),
        in_specs=[
            *[whole(own.shape)] * 8,
            pl.BlockSpec((d_model, TILE), lambda i: (0, i)),
            pl.BlockSpec((1, TILE), lambda i: (0, i)),
            pl.BlockSpec((d_model, TILE), lambda i: (0, i)),
        ],
        out_specs=[
            pl.BlockSpec((1, rows, TILE), lambda i: (i, 0, 0)),
            pl.BlockSpec((1, rows, TILE), lambda i: (i, 0, 0)),
            pl.BlockSpec((1, TILE), lambda i: (0, i)),
            whole((rows // 2, d_model)),
            whole((rows // 4, d_model)),
            whole((rows // 4, d_model)),
        ],
        out_shape=[
            shape_of((steps, rows, TILE), LOW),
            shape_of((steps, rows, TILE), LOW),
            shape_of((1, units), FULL),
            shape_of((rows // 2, d_model), FULL),
            shape_of((rows // 4, d_model), LOW),
            shape_of((rows // 4, d_model), LOW),
        ],
        scratch_shapes=[
            pltpu.VMEM((rows, d_model), LOW),
            pltpu.VMEM((rows, d_model), LOW),
            pltpu.VMEM((rows, d_model), FULL),
        ],
        compiler_params=params(48),
        cost_estimate=cost(20),
    )(own, near, far, last, *dy, w_up, b_up, w_down)


def gel_kernel(own, near, far, last, w_up, b_up, gel_out, act):
    @pl.when(pl.program_id(0) == 0)
    def _():
        stack_rows(act, (own, near, far, last))

    upper = dot(act[...], w_up[...], COLS) + b_up[...].astype(FULL)
    gel_out[0] = (upper * (0.5 + 0.5 * lax.erf(upper * (0.5**0.5)))).astype(LOW)


def gel_first(own, near, far, last, w_up, b_up, steps):
    d_model = own.shape[1]
    rows = 4 * own.shape[0]
    return pl.pallas_call(
        gel_kernel,
        grid=(steps,),
        in_specs=[
            *[whole(own.shape)] * 4,
            pl.BlockSpec((d_model, TILE), lambda i: (0, i)),
            pl.BlockSpec((1, TILE), lambda i: (0, i)),
        ],
        out_specs=pl.BlockSpec((1, rows, TILE), lambda i: (i, 0, 0)),
        out_shape=shape_of((steps, rows, TILE), LOW),
        scratch_shapes=[pltpu.VMEM((rows, d_model), LOW)],
        compiler_params=params(32),
        cost_estimate=cost(2 * steps),
    )(own, near, far, last, w_up, b_up)


def down_kernel(gel, w_down, keep_out, send_out, fold_out, total):
    step = pl.program_id(0)
    half = total.shape[0] // 2
    part = dot(gel[0], w_down[...], BOTH)

    @pl.when(step == 0)
    def _():
        total[...] = part

    @pl.when(step > 0)
    def _():
        total[...] += part

    @pl.when(step == pl.num_programs(0) - 1)
    def _():
        keep_out[...] = total[:half]
        send_out[...] = total[half : half + half // 2].astype(LOW)
        fold_out[...] = total[half + half // 2 :].astype(LOW)


def down_part(gel, w_down):
    d_model, units = w_down.shape
    rows = gel.shape[1]
    return pl.pallas_call(
        down_kernel,
        grid=(units // TILE,),
        in_specs=[
            pl.BlockSpec((1, rows, TILE), lambda i: (i, 0, 0)),
            pl.BlockSpec((d_model, TILE), lambda i: (0, i)),
        ],
        out_specs=[whole((rows // 2, d_model))] + [whole((rows // 4, d_model))] * 2,
        out_shape=[shape_of((rows // 2, d_model), FULL)] + [shape_of((rows // 4, d_model), LOW)] * 2,
        scratch_shapes=[pltpu.VMEM((rows, d_model), FULL)],
        compiler_params=params(40),
        cost_estimate=cost(7),
    )(gel, w_down)


def turn_kernel(keep, got, last, resid, dy, gain, dh_out, dattn_out, sum_out):
    da2 = keep[...] + got[...].astype(FULL) + last[...].astype(FULL)
    unit, inverse = normalize(resid[...])
    dy_full = dy[...].astype(FULL)
    dh = dy_full + norm_back(da2, unit, inverse, gain[...].astype(FULL))
    dh_out[...] = dh
    dattn = dh.astype(LOW)
    dattn_out[...] = dattn
    sum_out[0:1] = jnp.sum(da2 * unit, axis=0, keepdims=True)
    sum_out[1:2] = jnp.sum(da2, axis=0, keepdims=True)
    sum_out[2:3] = jnp.sum(dattn.astype(FULL), axis=0, keepdims=True)
    sum_out[3:4] = jnp.sum(dy_full, axis=0, keepdims=True)


def turn(keep, got, last, resid, dy, gain):
    dims = resid.shape
    return pl.pallas_call(
        turn_kernel,
        grid=(1,),
        in_specs=[whole(dims)] * 5 + [whole(gain.shape)],
        out_specs=[whole(dims), whole(dims), whole((4, dims[1]))],
        out_shape=[shape_of(dims, FULL), shape_of(dims, LOW), shape_of((4, dims[1]), FULL)],
        compiler_params=params(24),
        cost_estimate=cost(3),
    )(keep, got, last, resid, dy, gain)


def back_kernel(scale, own, near, far, last, w_out, qkv, probs_in, w_qkv, dqkv_out, sum_out, keep_out, send_out, fold_out, act, total):
    step = pl.program_id(0)
    half = act.shape[0] // 2

    @pl.when(step == 0)
    def _():
        stack_rows(act, (own, near, far, last))
        total[...] = jnp.zeros_like(total)

    dmixed = dot(act[...], w_out[...], COLS).astype(LOW)
    for h in range(w_out.shape[1] // DH):
        at = slice(h * DH, (h + 1) * DH)
        probs = probs_in[h]
        dm = dmixed[:, at]
        dqkv_out[2, :, at] = dot(probs.astype(LOW), dm, ROWS).astype(LOW)
        dprobs = dot(dm, qkv[2, :, at], BOTH)
        terms = jnp.sum(probs * dprobs, axis=-1, keepdims=True)
        ds = (probs * (dprobs - terms) * scale).astype(LOW)
        dqkv_out[0, :, at] = dot(ds, qkv[1, :, at], COLS).astype(LOW)
        dqkv_out[1, :, at] = dot(ds, qkv[0, :, at], ROWS).astype(LOW)
    part = dot(dqkv_out[0], w_qkv[0], BOTH)
    part += dot(dqkv_out[1], w_qkv[1], BOTH)
    part += dot(dqkv_out[2], w_qkv[2], BOTH)
    total[...] += part
    for row, t in enumerate((0, 2)):
        sum_out[row : row + 1] = jnp.sum(dqkv_out[t].astype(FULL), axis=0, keepdims=True)

    @pl.when(step == pl.num_programs(0) - 1)
    def _():
        keep_out[...] = total[:half]
        send_out[...] = total[half : half + half // 2].astype(LOW)
        fold_out[...] = total[half + half // 2 :].astype(LOW)


def attention_back(own, near, far, last, w_out, qkv, probs, w_qkv, group=2):
    d_model, width = w_out.shape
    rows = qkv.shape[1]
    cols = group * DH
    return pl.pallas_call(
        functools.partial(back_kernel, DH**-0.5),
        grid=(width // cols,),
        in_specs=[
            *[whole(own.shape)] * 4,
            pl.BlockSpec((d_model, cols), lambda i: (0, i)),
            pl.BlockSpec((3, rows, cols), lambda i: (0, 0, i)),
            pl.BlockSpec((group, rows, rows), lambda i: (i, 0, 0)),
            pl.BlockSpec((3, d_model, cols), lambda i: (0, 0, i)),
        ],
        out_specs=[
            pl.BlockSpec((3, rows, cols), lambda i: (0, 0, i)),
            pl.BlockSpec((2, cols), lambda i: (0, i)),
            whole((rows // 2, d_model)),
            whole((rows // 4, d_model)),
            whole((rows // 4, d_model)),
        ],
        out_shape=[
            shape_of((3, rows, width), LOW),
            shape_of((2, width), FULL),
            shape_of((rows // 2, d_model), FULL),
            shape_of((rows // 4, d_model), LOW),
            shape_of((rows // 4, d_model), LOW),
        ],
        scratch_shapes=[pltpu.VMEM((rows, d_model), LOW), pltpu.VMEM((rows, d_model), FULL)],
        compiler_params=params(48),
        cost_estimate=cost(15),
    )(own, near, far, last, w_out, qkv, probs, w_qkv)


def leave_kernel(keep, got, last, x_own, dh, gain, grad_out, sum_out):
    da1 = keep[...] + got[...].astype(FULL) + last[...].astype(FULL)
    unit, inverse = normalize(x_own[...].astype(FULL))
    grad_out[...] = (dh[...] + norm_back(da1, unit, inverse, gain[...].astype(FULL))).astype(LOW)
    sum_out[0:1] = jnp.sum(da1 * unit, axis=0, keepdims=True)
    sum_out[1:2] = jnp.sum(da1, axis=0, keepdims=True)


def leave(keep, got, last, x_own, dh, gain):
    dims = x_own.shape
    return pl.pallas_call(
        leave_kernel,
        grid=(1,),
        in_specs=[whole(dims)] * 5 + [whole(gain.shape)],
        out_specs=[whole(dims), whole((2, dims[1]))],
        out_shape=[shape_of(dims, LOW), shape_of((2, dims[1]), FULL)],
        compiler_params=params(24),
        cost_estimate=cost(2.5),
    )(keep, got, last, x_own, dh, gain)


def place_kernel(items, mp, sub, spot, own, near, far, last, out):
    for at, source in enumerate((own, near, far, last)):
        for s in range(items):
            rows = slice(s * sub, (s + 1) * sub)
            out[spot[s], spot[items + at]] = source[rows, :].astype(out.dtype)


def place(own, near, far, last, spot, items, mp, kind):
    rows, d_model = own.shape
    sub = rows // items
    return pl.pallas_call(
        functools.partial(place_kernel, items, mp, sub),
        in_specs=[pl.BlockSpec(memory_space=pltpu.SMEM)] + [pl.BlockSpec(memory_space=pltpu.VMEM)] * 4,
        out_specs=pl.BlockSpec(memory_space=pltpu.VMEM),
        out_shape=shape_of((items, mp, sub, d_model), kind),
        compiler_params=params(24),
        cost_estimate=cost(3),
    )(spot, own, near, far, last).reshape(items, mp * sub, d_model)


def product_kernel(shifts, n_units, spots, *refs):
    units = refs[len(refs) - n_units - 1 : -1]
    out = refs[-1]
    for at in range(shifts):
        columns = refs[at * n_units : (at + 1) * n_units]
        part = sum(dot(c[...], u[0], ROWS) for c, u in zip(columns, units))
        rows = part.shape[0]
        out[0, at * rows : (at + 1) * rows] = part.astype(LOW)


def add_kernel(n_units, spots, *refs):
    columns, units = refs[:n_units], refs[n_units : 2 * n_units]
    got, out = refs[2 * n_units :]
    part = sum(dot(c[...], u[0], ROWS) for c, u in zip(columns, units))
    out[0] = (part + got[0].astype(FULL)).astype(LOW)


def products(kernel, blocks, chunk, spots, columns, units, tiles, more=()):
    rows, first, steps = units[0].shape[1], tiles[0], len(tiles)
    in_specs, args = [], []
    for k in blocks:
        for array, base in columns:
            in_specs.append(pl.BlockSpec((rows, chunk), lambda i, spots, at=base + k: (0, spots[at])))
            args.append(array)
    for array in units:
        start = first if array.shape[0] != steps else 0
        in_specs.append(pl.BlockSpec((1, rows, TILE), lambda i, spots, start=start: (start + i, 0, 0)))
        args.append(array)
    for array, block in more:
        in_specs.append(pl.BlockSpec((1, chunk, TILE), lambda i, spots, block=block: (i, block, 0)))
        args.append(array)
    size = chunk * len(blocks)
    return pl.pallas_call(
        kernel,
        grid_spec=pltpu.PrefetchScalarGridSpec(
            num_scalar_prefetch=1,
            grid=(steps,),
            in_specs=in_specs,
            out_specs=pl.BlockSpec((1, size, TILE), lambda i, spots: (i, 0, 0)),
        ),
        out_shape=shape_of((steps, size, TILE), LOW),
        compiler_params=params(32),
        cost_estimate=cost(0.6 * steps * len(blocks)),
    )(spots, *args)


def pass_kernel(mine, got, out):
    out[...] = (mine[...].astype(FULL) + got[...].astype(FULL)).astype(LOW)


def pass_on(got, mine, chunk):
    steps = mine.shape[0]
    tail = pl.BlockSpec((1, chunk, TILE), lambda i, j: (i, 1 + j, 0))
    return pl.pallas_call(
        pass_kernel,
        grid=(steps, 2),
        in_specs=[tail, tail],
        out_specs=pl.BlockSpec((1, chunk, TILE), lambda i, j: (i, j, 0)),
        out_shape=shape_of((steps, 2 * chunk, TILE), LOW),
        compiler_params=params(16),
        cost_estimate=cost(steps),
    )(mine, got)


def finish_kernel(inner, mine, got, across, near, last, *refs):
    out = refs[-1]

    @pl.when(inner[0] == 1)
    def _():
        out[...] = (mine[...].astype(FULL) + got[...].astype(FULL) + across[...].astype(FULL)).reshape(out.shape)

    @pl.when(inner[0] == 0)
    def _():
        out[...] = (near[...].astype(FULL) + last[...].astype(FULL)).reshape(out.shape)


def finish(last, inner, mine, got, across, near, tiles, total, split, before):
    steps, chunk, _ = near.shape
    first = tiles[0]
    head = pl.BlockSpec((1, chunk, TILE), lambda i: (i, 0, 0))
    in_specs = [pl.BlockSpec(memory_space=pltpu.SMEM)] + [head] * 5
    args = [inner, mine, got, across, near, last]
    aliases = {}
    if before is not None:
        in_specs.append(pl.BlockSpec(memory_space=pl.ANY))
        args.append(before)
        aliases = {6: 0}
    if split:
        out_spec = pl.BlockSpec((1, chunk, TILE), lambda i: (first + i, 0, 0))
        out_shape = shape_of((total, chunk, TILE), FULL)
    else:
        out_spec = pl.BlockSpec((chunk, TILE), lambda i: (0, first + i))
        out_shape = shape_of((chunk, total * TILE), FULL)
    return pl.pallas_call(
        finish_kernel,
        grid=(steps,),
        in_specs=in_specs,
        out_specs=out_spec,
        out_shape=out_shape,
        input_output_aliases=aliases,
        compiler_params=params(16),
        cost_estimate=cost(steps),
    )(*args)


def on_device(
    dp,
    blk,
    mp,
    inputs,
    lengths,
    w_qkv,
    b_qv,
    w_out,
    out_biases,
    ln_gains,
    ln_shifts,
    w_up,
    b_up,
    w_down,
    cotangent,
):
    items, block_len, d_model = inputs.shape
    width = w_qkv.shape[2]
    sub = block_len // mp
    own_rows = blk * sub
    rows = own_rows * mp
    chunk = d_model // (dp * blk)
    half_cols = blk * chunk
    paired = dp == 2
    order = Order()
    x, z, me = lax.axis_index("dp"), lax.axis_index("blk"), lax.axis_index("mp")

    def to_items(array):
        mine = lax.dynamic_slice_in_dim(array, me * sub, sub, axis=1)
        parts = [lax.dynamic_index_in_dim(mine, z, 0, keepdims=False)]
        for s in range(1, blk):
            piece = lax.dynamic_index_in_dim(mine, lax.rem(z + s, blk), 0, keepdims=False)
            parts.append(lax.ppermute(piece, "blk", shift(blk, s)))
        return parts

    def swap_core(array):
        return lax.ppermute(array, "mp", flip(mp, 1))

    def swap_y(array):
        return lax.ppermute(array, "mp", flip(mp, 2))

    def swap_dp(array):
        return lax.ppermute(array, "dp", flip(dp, 1))

    def join(parts):
        return jnp.concatenate(parts, axis=0)

    def gather_mp(own):
        near = swap_y(own)
        return own, near, swap_core(own), swap_core(near)

    spot = jnp.stack(
        [lax.rem(z + s, blk) for s in range(blk)] + [me ^ j for j in (0, 2, 1, 3)]
    ).astype(jnp.int32)

    def from_items(own):
        parts = [own[:sub]]
        for s in range(1, blk):
            parts.append(lax.ppermute(own[s * sub : (s + 1) * sub], "blk", shift(blk, -s)))
        return join(parts)

    in_block = jnp.arange(sub, dtype=jnp.int32)
    block_of = lax.rem(z - jnp.arange(blk, dtype=jnp.int32) + blk, blk)

    def positions_of(q):
        return (block_of[:, None] * block_len + q * sub + in_block[None, :]).reshape(-1)

    pos = jnp.concatenate([positions_of(me ^ j) for j in (0, 2, 1, 3)])
    length = lax.dynamic_slice_in_dim(lengths, z, 1)

    def other_half(array):
        return lax.dynamic_slice_in_dim(array, (1 - x) * half_cols, half_cols, axis=1)

    line = [jnp.where(z < blk // 2, k, blk - 1 - k) for k in range(blk)]
    inner = jnp.where((z == 0) | (z == blk - 1), 0, 1).astype(jnp.int32)[None]
    spots = jnp.stack(
        [x * blk + at for at in line] + line + [blk + at for at in line]
    ).astype(jnp.int32)
    to_inner, across, to_end = [(0, 1), (3, 2)], [(1, 2), (2, 1)], [(1, 0), (2, 3)]

    class Piece:
        def __init__(self, columns, units, tiles):
            self.args = (chunk, spots, columns, units, tiles)
            self.tiles = tiles

        def start(self, needs=()):
            kernel = functools.partial(product_kernel, blk - 1, len(self.args[3]))
            self.mine = order.run(lambda first: products(kernel, (1, 2, 3), chunk, spots, [(first, self.args[2][0][1])] + self.args[2][1:], self.args[3], self.tiles), self.args[2][0][0], needs=needs)
            self.got = lax.ppermute(self.mine, "blk", to_inner)

        def cross(self, needs=()):
            send = order.run(pass_on, self.got, self.mine, chunk, needs=needs)
            self.across = lax.ppermute(send, "blk", across)

        def back(self):
            kernel = functools.partial(add_kernel, len(self.args[3]))
            self.near = order.run(lambda got: products(kernel, (0,), chunk, spots, self.args[2], self.args[3], self.tiles, [(got, 1)]), self.across)
            self.last = lax.ppermute(self.near, "blk", to_end)

        def end(self, total, split=False, before=None):
            return order.run(finish, self.last, inner, self.mine, self.got, self.across, self.near, self.tiles, total, split, before)

    def grad_plain(full, unit):
        part = jnp.einsum("rd,trc->dtc", full, unit, preferred_element_type=FULL).astype(LOW)
        part = lax.psum_scatter(part, ("dp", "blk"), scatter_dimension=0, tiled=True)
        return part.astype(FULL)

    w_three = w_qkv.transpose(1, 0, 2)
    b_three = jnp.stack([b_qv[0], jnp.zeros_like(b_qv[0]), b_qv[1]]).astype(FULL)
    gain_one, gain_two = ln_gains[:1], ln_gains[1:]
    shift_one, shift_two = ln_shifts[:1], ln_shifts[1:]

    def sum_over(array, axis, size):
        bit = 1
        while bit < size:
            array = array + lax.ppermute(array, axis, flip(size, bit))
            bit *= 2
        return array

    x_own, act_one_own = enter(gain_one, shift_one, to_items(inputs))
    order.last = act_one_own
    act_one_parts = gather_mp(act_one_own)
    valid = (pos[:own_rows] < length).astype(LOW)[:, None]
    dy_own = join(to_items(cotangent)) * valid
    dy_near = swap_y(after(dy_own, act_one_parts[1]))
    qkv, probs, mixed, keep, got, fold_got = order.run(
        attention, act_one_parts[0], *act_one_parts[1:], w_three, b_three, w_out, pos, length, needs=[dy_own]
    )
    got, fold_got = swap_core(got), swap_core(fold_got)
    if paired:
        halves_one = swap_dp(jnp.concatenate([other_half(act_one_own), other_half(dy_own)], axis=1))
        mixed_other = swap_dp(after(mixed, halves_one))
    last = swap_y(order.run(fold, fold_got, keep, needs=[dy_near]))
    dy_parts = dy_own, dy_near, swap_core(dy_own), swap_core(dy_near)
    resid, act_two_own = order.run(middle, x_own, keep, got, last, out_biases, gain_two, shift_two, needs=dy_parts)
    act_two_parts = gather_mp(act_two_own)
    tiles = w_up.shape[1] // TILE
    some = tiles // 2
    b_row = b_up[None]
    needs = []
    if paired:
        halves_near = swap_y(after(halves_one, act_two_parts[1]))
        needs = [mixed_other]
    gel_part = order.run(gel_first, act_two_parts[0], *act_two_parts[1:], w_up, b_row, some, needs=needs)
    if paired:
        gel_part_other = swap_dp(gel_part)
    gel, dup, up_sum, keep, got, fold_got = order.run(
        feed, act_two_parts[0], *act_two_parts[1:], dy_parts, w_up, b_row, w_down
    )
    got, fold_got = swap_core(got), swap_core(fold_got)
    dy = join(dy_parts)
    needs = []
    if paired:
        halves_one = join([halves_one, halves_near, swap_core(halves_one), swap_core(halves_near)])
        gel_rest_other = swap_dp(gel[some:])
        needs = [halves_one]
    last = swap_y(order.run(fold, fold_got, keep, needs=needs))
    da2 = keep, got, last
    if paired:
        columns = [(dy, 0), (halves_one, 2 * blk)]
        g0 = Piece(columns, [gel_part, gel_part_other], list(range(some)))
        g1 = Piece(columns, [gel, gel_rest_other], list(range(some, tiles)))
        g0.start()
    down_keep, down_got, down_fold = order.run(down_part, gel, w_down)
    down_got, down_fold = swap_core(down_got), swap_core(down_fold)
    dh, dattn_own, sums_two = order.run(turn, da2[0], *da2[1:], resid, dy_own, gain_two)
    dattn_parts = gather_mp(dattn_own)
    if paired:
        halves_two = swap_dp(
            after(
                jnp.concatenate([other_half(act_two_own), other_half(dattn_own)], axis=1),
                gel_rest_other,
            )
        )
        g1.start()
        dup_part_other = swap_dp(after(dup[:some], halves_two))
    down_near = order.run(fold, down_fold, down_keep)
    down_last = swap_y(after(down_near, dattn_parts[1]))
    needs = []
    if paired:
        halves_near = swap_y(after(halves_two, dattn_parts[1]))
        needs = [halves_two, g0.got]
    dqkv, qkv_sum, keep, got, fold_got = order.run(
        attention_back, dattn_parts[0], *dattn_parts[1:], w_out, qkv, probs, w_three, needs=needs
    )
    got, fold_got = swap_core(got), swap_core(fold_got)
    act_one, act_two, dattn = join(act_one_parts), join(act_two_parts), join(dattn_parts)
    needs = []
    if paired:
        halves_two = join([halves_two, halves_near, swap_core(halves_two), swap_core(halves_near)])
        columns = [(act_two, 0), (halves_two, blk)]
        u0 = Piece(columns, [dup, dup_part_other], list(range(some)))
        g0.cross()
        u0.start(needs=[halves_near])
        dup_rest_other = swap_dp(after(dup[some:], dup_part_other))
        u1 = Piece(columns, [dup, dup_rest_other], list(range(some, tiles)))
        dqkv_other = swap_dp(after(dqkv, dup_rest_other))
        needs = [g1.got]
    last = swap_y(order.run(fold, fold_got, keep))
    da1 = keep, got, last
    output = order.run(output_of, down_last, down_keep, down_got, resid, out_biases)
    output = from_items(output)
    input_grad, sums_one = order.run(leave, da1[0], *da1[1:], x_own, dh, gain_one, needs=needs)
    input_grad = from_items(input_grad)
    sums = jnp.concatenate([sums_one, sums_two], axis=0).reshape(-1)
    sums = sum_over(sums, "mp", mp)
    sums = jnp.concatenate([sums, qkv_sum.reshape(-1), up_sum.reshape(-1)])
    output = gather_mp(output)
    input_grad = gather_mp(input_grad)
    if paired:
        g1.cross()
        g0.back()
        u1.start()
        grad_down = g0.end(tiles)
    output = order.run(place, output[0], *output[1:], spot, items, mp, LOW)
    sums = sums + lax.ppermute(sums, "blk", flip(blk, 1))
    if paired:
        g1.back()
        columns = [(act_one, 0), (halves_one, blk)]
        q0 = Piece(columns, [dqkv, dqkv_other], [0, 1])
        q1 = Piece(columns, [dqkv, dqkv_other], [2])
        q0.start(needs=[u0.got, sums])
        u0.cross()
        grad_down = g1.end(tiles, before=grad_down)
    sums = sums + lax.ppermute(sums, "blk", flip(blk, 2))
    input_grad = order.run(place, input_grad[0], *input_grad[1:], spot, items, mp, FULL)
    if paired:
        q1.start()
        columns = [(dattn, 0), (halves_two, 2 * blk)]
        o0 = Piece(columns, [mixed[None], mixed_other[None]], [0])
        o0.start(needs=[u1.got, sums])
    sums = sum_over(sums, "dp", dp)
    if paired:
        u1.cross()
        u0.back()
        grad_up = u0.end(tiles)
        q0.cross(needs=[sums])
        u1.back()
        grad_up = u1.end(tiles, before=grad_up)
        q1.cross()
        q0.back()
        o0.cross()
        q1.back()
        grad_qkv = q0.end(3, True)
        o0.back()
        grad_qkv = q1.end(3, True, before=grad_qkv).transpose(1, 0, 2)
        grad_out = o0.end(1)
    else:
        grad_down = grad_plain(dy, gel).reshape(chunk, -1)
        grad_up = grad_plain(act_two, dup).reshape(chunk, -1)
        grad_out = grad_plain(dattn, mixed[None]).reshape(chunk, -1)
        grad_qkv = grad_plain(act_one, dqkv)

    per_token = sums[: 6 * d_model].reshape(6, d_model)
    grad_qv_bias = sums[6 * d_model : 6 * d_model + 2 * width].reshape(2, width)
    return (
        output,
        input_grad,
        grad_qkv,
        grad_qv_bias,
        grad_out,
        per_token[4:6],
        jnp.stack([per_token[0], per_token[2]]),
        jnp.stack([per_token[1], per_token[3]]),
        grad_up,
        sums[6 * d_model + 2 * width :],
        grad_down,
    )


def solution(mesh):
    sizes = [mesh.shape[name] for name in ("dp", "blk", "mp")]
    in_specs = (
        P("dp", "blk", None),
        P("dp"),
        P(None, None, "mp"),
        P(None, "mp"),
        P(None, "mp"),
        P(),
        P(),
        P(),
        P(None, "mp"),
        P("mp"),
        P(None, "mp"),
        P("dp", "blk", None),
    )
    out_specs = (
        P("dp", "blk", None),
        P("dp", "blk", None),
        P(("dp", "blk"), None, "mp"),
        P(None, "mp"),
        P(("dp", "blk"), "mp"),
        P(),
        P(),
        P(),
        P(("dp", "blk"), "mp"),
        P("mp"),
        P(("dp", "blk"), "mp"),
    )

    def step(*arrays):
        return on_device(*sizes, *arrays)

    return jax.shard_map(
        step, mesh=mesh, in_specs=in_specs, out_specs=out_specs, check_vma=False
    )
```

```python
import functools

import jax
import jax.numpy as jnp
from jax import lax
from jax.experimental import pallas as pl
from jax.experimental.pallas import tpu as pltpu
from jax.sharding import PartitionSpec as P

DH = 128
LOW = jnp.bfloat16
FULL = jnp.float32
TILE = 512
BAND = 32


def flip(size, bit):
    return [(i, i ^ bit) for i in range(size)]


def shift(size, step):
    return [(i, (i + step) % size) for i in range(size)]


def after(value, *others):
    return lax.optimization_barrier((value, *others))[0]


class Order:
    def __init__(self):
        self.last = None
        self.needs = ()

    def run(self, function, first, *others):
        waits = list(self.needs) + ([] if self.last is None else [self.last])
        if waits:
            first = after(first, *waits)
        results = function(first, *others)
        self.last = results[-1] if isinstance(results, (list, tuple)) else results
        self.needs = ()
        return results


def dot(left, right, dims):
    return lax.dot_general(left, right, (dims, ((), ())), preferred_element_type=FULL)


COLS = ((1,), (0,))
BOTH = ((1,), (1,))
ROWS = ((0,), (0,))


def shape_of(dims, kind):
    return jax.ShapeDtypeStruct(dims, kind)


def whole(dims):
    return pl.BlockSpec(dims, lambda *_: (0,) * len(dims))


def params(megabytes):
    return pltpu.CompilerParams(vmem_limit_bytes=megabytes << 20)


def cost(microseconds, share=0.05):
    flops = int(microseconds * share * 1153.5e6)
    return pl.CostEstimate(flops=flops, bytes_accessed=1, transcendentals=0)


def give_rows(values, targets):
    at = 0
    for target in targets:
        target[...] = values[at : at + target.shape[0]]
        at += target.shape[0]


def stack_rows(target, pieces):
    at = 0
    for piece in pieces:
        target[at : at + piece.shape[0], :] = piece[...]
        at += piece.shape[0]


def normalize(values):
    centered = values - jnp.mean(values, axis=-1, keepdims=True)
    variance = jnp.mean(centered * centered, axis=-1, keepdims=True)
    inverse = lax.rsqrt(variance + 1e-05)
    return centered * inverse, inverse


def norm_back(grad_norm, unit, inverse, gain):
    scaled = grad_norm * gain
    first = jnp.mean(scaled, axis=-1, keepdims=True)
    second = jnp.mean(scaled * unit, axis=-1, keepdims=True)
    return inverse * (scaled - first - unit * second)


def enter_kernel(first, gain, bias, *refs):
    pieces, (x_out, act_out) = (first, *refs[:-2]), refs[-2:]
    stack_rows(x_out, pieces)
    unit, _ = normalize(x_out[...].astype(FULL))
    act_out[...] = (unit * gain[...].astype(FULL) + bias[...].astype(FULL)).astype(LOW)


def enter(first, gain, bias, *others):
    rows, d_model = (1 + len(others)) * first.shape[0], first.shape[1]
    return pl.pallas_call(
        enter_kernel,
        out_shape=[shape_of((rows, d_model), LOW)] * 2,
        compiler_params=params(12),
        cost_estimate=cost(2),
    )(first, gain, bias, *others)


def mask_kernel(first, length, pos, *refs):
    pieces, out = (first, *refs[:-1]), refs[-1]
    stack_rows(out, pieces)
    out[...] = out[...] * (pos[...] < length[0]).astype(LOW)


def masked(first, length, pos, *others):
    rows, d_model = (1 + len(others)) * first.shape[0], first.shape[1]
    vmem = pl.BlockSpec(memory_space=pltpu.VMEM)
    return pl.pallas_call(
        mask_kernel,
        in_specs=[vmem, pl.BlockSpec(memory_space=pltpu.SMEM)] + [vmem] * (1 + len(others)),
        out_shape=shape_of((rows, d_model), LOW),
        compiler_params=params(12),
        cost_estimate=cost(1),
    )(first, length, pos, *others)


def attention_kernel(scale, own, near, far, last, w_qkv, b_qkv, w_out, pos_row, pos_col, length, qkv_out, probs_out, mixed_out, keep_out, send_out, fold_out, fold_last, act, bias, total):
    step = pl.program_id(0)
    half = act.shape[0] // 2

    @pl.when(step == 0)
    def _():
        stack_rows(act, (own, near, far, last))
        allowed = (pos_row[...] <= pos_col[...]) & (pos_row[...] < length[0])
        bias[...] = jnp.where(allowed, 0.0, -1e30)
        total[...] = jnp.zeros_like(total)

    for t in range(3):
        qkv_out[t] = (dot(act[...], w_qkv[t], COLS) + b_qkv[t][None]).astype(LOW)
    for h in range(w_out.shape[1] // DH):
        at = slice(h * DH, (h + 1) * DH)
        scores = dot(qkv_out[0, :, at], qkv_out[1, :, at], BOTH) * scale + bias[...]
        expo = jnp.exp(scores - jnp.max(scores, axis=-1, keepdims=True))
        probs = expo * (1.0 / jnp.sum(expo, axis=-1, keepdims=True))
        probs_out[h] = probs
        mixed_out[:, at] = dot(probs.astype(LOW), qkv_out[2, :, at], COLS).astype(LOW)
    total[...] += dot(mixed_out[...], w_out[...], BOTH)

    @pl.when(step == pl.num_programs(0) - 1)
    def _():
        keep_out[...] = total[:half]
        send_out[...] = total[half : half + half // 2].astype(LOW)
        give_rows(total[half + half // 2 :].astype(LOW), (fold_out, fold_last))


def attention(own, near, far, last, w_qkv, b_qkv, w_out, pos, length, group=2):
    d_model, width = w_out.shape
    rows = 4 * own.shape[0]
    cols = group * DH
    heads = width // DH
    return pl.pallas_call(
        functools.partial(attention_kernel, DH**-0.5),
        grid=(width // cols,),
        in_specs=[
            *[whole(own.shape)] * 4,
            pl.BlockSpec((3, d_model, cols), lambda i: (0, 0, i)),
            pl.BlockSpec((3, cols), lambda i: (0, i)),
            pl.BlockSpec((d_model, cols), lambda i: (0, i)),
            whole((1, rows)),
            whole((rows, 1)),
            pl.BlockSpec(memory_space=pltpu.SMEM),
        ],
        out_specs=[
            pl.BlockSpec((3, rows, cols), lambda i: (0, 0, i)),
            pl.BlockSpec((group, rows, rows), lambda i: (i, 0, 0)),
            pl.BlockSpec((rows, cols), lambda i: (0, i)),
            whole((rows // 2, d_model)),
            whole((rows // 4, d_model)),
            *[whole((rows // 8, d_model))] * 2,
        ],
        out_shape=[
            shape_of((3, rows, width), LOW),
            shape_of((heads, rows, rows), FULL),
            shape_of((rows, width), LOW),
            shape_of((rows // 2, d_model), FULL),
            shape_of((rows // 4, d_model), LOW),
            *[shape_of((rows // 8, d_model), LOW)] * 2,
        ],
        scratch_shapes=[
            pltpu.VMEM((rows, d_model), LOW),
            pltpu.VMEM((rows, rows), FULL),
            pltpu.VMEM((rows, d_model), FULL),
        ],
        compiler_params=params(48),
        cost_estimate=cost(14),
    )(own, near, far, last, w_qkv, b_qkv, w_out, pos[None, :], pos[:, None], length)


def fold_kernel(got, last, keep, out):
    half = got.shape[0]
    out[:half] = (keep[:half] + got[...].astype(FULL)).astype(LOW)
    out[half:] = (keep[half:] + last[...].astype(FULL)).astype(LOW)


def fold(got, last, keep):
    rows, d_model = 2 * got.shape[0], got.shape[1]
    return pl.pallas_call(
        fold_kernel,
        grid=(1,),
        in_specs=[whole(got.shape)] * 2 + [pl.BlockSpec((rows, d_model), lambda i: (1, 0))],
        out_specs=whole((rows, d_model)),
        out_shape=shape_of((rows, d_model), LOW),
        compiler_params=params(12),
        cost_estimate=cost(1),
    )(got, last, keep)


def middle_kernel(x_own, keep, got, last, biases, gain, bias, resid_out, act_out):
    attn = keep[...] + got[...].astype(FULL) + last[...].astype(FULL) + biases[:1].astype(FULL)
    resid = x_own[...].astype(FULL) + attn
    resid_out[...] = resid
    unit, _ = normalize(resid)
    act_out[...] = (unit * gain[...].astype(FULL) + bias[...].astype(FULL)).astype(LOW)


def middle(x_own, keep, got, last, biases, gain, bias):
    dims = x_own.shape
    block = pl.BlockSpec((BAND, dims[1]), lambda i: (i, 0))
    return pl.pallas_call(
        middle_kernel,
        grid=(dims[0] // BAND,),
        in_specs=[block] * 4 + [whole(biases.shape), whole(gain.shape), whole(bias.shape)],
        out_specs=[block] * 2,
        out_shape=[shape_of(dims, FULL), shape_of(dims, LOW)],
        compiler_params=params(12),
        cost_estimate=cost(2),
    )(x_own, keep, got, last, biases, gain, bias)


def feed_kernel(closing, own, near, far, last, dy_own, dy_near, dy_far, dy_last, w_up, b_up, w_down, *rest):
    gel_out, dup_out, sum_out = rest[closing : closing + 3]
    act, dy, total = rest[-3:]
    step = pl.program_id(0)
    half = act.shape[0] // 2

    @pl.when(step == 0)
    def _():
        stack_rows(act, (own, near, far, last))
        stack_rows(dy, (dy_own, dy_near, dy_far, dy_last))
        total[...] = rest[0][...] if closing else jnp.zeros_like(total)

    upper = dot(act[...], w_up[...], COLS) + b_up[...].astype(FULL)
    dgel = dot(dy[...], w_down[...], COLS)
    phi = 0.5 + 0.5 * lax.erf(upper * (0.5**0.5))
    gel_out[0] = (upper * phi).astype(LOW)
    slope = phi + upper * jnp.exp(-0.5 * upper * upper) * 0.3989422804014327
    dup = (dgel * slope).astype(LOW)
    dup_out[0] = dup
    sum_out[...] = jnp.sum(dup.astype(FULL), axis=0, keepdims=True)
    total[...] += dot(dup, w_up[...], BOTH)

    @pl.when(step == pl.num_programs(0) - 1)
    def _():
        if closing:
            keep_out, send_out, fold_out, fold_last = rest[4:8]
            keep_out[...] = total[:half]
            send_out[...] = total[half : half + half // 2].astype(LOW)
            give_rows(total[half + half // 2 :].astype(LOW), (fold_out, fold_last))
        else:
            rest[3][...] = total[...]


def feed(own, near, far, last, dy, w_up, b_up, w_down, before, first, steps):
    d_model = own.shape[1]
    rows = 4 * own.shape[0]
    closing = before is not None
    out_specs = [pl.BlockSpec((1, rows, TILE), lambda i: (i, 0, 0))] * 2
    out_specs.append(pl.BlockSpec((1, TILE), lambda i: (0, i)))
    out_shape = [shape_of((steps, rows, TILE), LOW)] * 2 + [shape_of((1, steps * TILE), FULL)]
    if closing:
        ends = [((rows // 2, d_model), FULL)]
        ends += [((rows // at, d_model), LOW) for at in (4, 8, 8)]
    else:
        ends = [((rows, d_model), FULL)]
    return pl.pallas_call(
        functools.partial(feed_kernel, int(closing)),
        grid=(steps,),
        in_specs=[
            *[whole(own.shape)] * 8,
            pl.BlockSpec((d_model, TILE), lambda i: (0, first + i)),
            pl.BlockSpec((1, TILE), lambda i: (0, first + i)),
            pl.BlockSpec((d_model, TILE), lambda i: (0, first + i)),
        ]
        + [whole((rows, d_model))] * closing,
        out_specs=out_specs + [whole(dims) for dims, _ in ends],
        out_shape=out_shape + [shape_of(*end) for end in ends],
        scratch_shapes=[
            pltpu.VMEM((rows, d_model), LOW),
            pltpu.VMEM((rows, d_model), LOW),
            pltpu.VMEM((rows, d_model), FULL),
        ],
        compiler_params=params(58),
        cost_estimate=cost(11, 1.0 if closing else 0.5),
    )(own, near, far, last, *dy, w_up, b_up, w_down, *([before] if closing else []))


def down_kernel(gel_first, gel_rest, w_down, keep_out, send_out, fold_out, fold_last, total):
    step = pl.program_id(0)
    half = total.shape[0] // 2

    @pl.when(step == 0)
    def _():
        total[...] = jnp.zeros_like(total)

    @pl.when(step < pl.num_programs(0) // 2)
    def _():
        total[...] += dot(gel_first[0], w_down[...], BOTH)

    @pl.when(step >= pl.num_programs(0) // 2)
    def _():
        total[...] += dot(gel_rest[0], w_down[...], BOTH)

    @pl.when(step == pl.num_programs(0) - 1)
    def _():
        keep_out[...] = total[:half]
        send_out[...] = total[half : half + half // 2].astype(LOW)
        give_rows(total[half + half // 2 :].astype(LOW), (fold_out, fold_last))


def down_part(gel_first, gel_rest, w_down):
    d_model, units = w_down.shape
    rows = gel_first.shape[1]
    half = units // TILE // 2
    return pl.pallas_call(
        down_kernel,
        grid=(units // TILE,),
        in_specs=[
            pl.BlockSpec((1, rows, TILE), lambda i: (jnp.minimum(i, half - 1), 0, 0)),
            pl.BlockSpec((1, rows, TILE), lambda i: (jnp.maximum(i - half, 0), 0, 0)),
            pl.BlockSpec((d_model, TILE), lambda i: (0, i)),
        ],
        out_specs=[whole((rows // at, d_model)) for at in (2, 4, 8, 8)],
        out_shape=[shape_of((rows // 2, d_model), FULL)]
        + [shape_of((rows // at, d_model), LOW) for at in (4, 8, 8)],
        scratch_shapes=[pltpu.VMEM((rows, d_model), FULL)],
        compiler_params=params(58),
        cost_estimate=cost(7),
    )(gel_first, gel_rest, w_down)


def add_rows(out, rows):
    @pl.when(pl.program_id(0) == 0)
    def _():
        out[...] = jnp.zeros_like(out)

    for at, row in enumerate(rows):
        out[at : at + 1] += jnp.sum(row, axis=0, keepdims=True)


def turn_kernel(keep, got, last, resid, dy, gain, dh_out, dattn_out, sum_out):
    da2 = keep[...] + got[...].astype(FULL) + last[...].astype(FULL)
    unit, inverse = normalize(resid[...])
    dy_full = dy[...].astype(FULL)
    dh = dy_full + norm_back(da2, unit, inverse, gain[...].astype(FULL))
    dh_out[...] = dh
    dattn = dh.astype(LOW)
    dattn_out[...] = dattn
    add_rows(sum_out, (da2 * unit, da2, dattn.astype(FULL), dy_full))


def turn(keep, got, last, resid, dy, gain):
    dims = resid.shape
    block = pl.BlockSpec((BAND, dims[1]), lambda i: (i, 0))
    return pl.pallas_call(
        turn_kernel,
        grid=(dims[0] // BAND,),
        in_specs=[block] * 5 + [whole(gain.shape)],
        out_specs=[block, block, whole((4, dims[1]))],
        out_shape=[shape_of(dims, FULL), shape_of(dims, LOW), shape_of((4, dims[1]), FULL)],
        compiler_params=params(12),
        cost_estimate=cost(3),
    )(keep, got, last, resid, dy, gain)


def back_kernel(scale, own, near, far, last, w_out, qkv, probs_in, w_qkv, dqkv_out, sum_out, keep_out, send_out, fold_out, fold_last, act, total):
    step = pl.program_id(0)
    half = act.shape[0] // 2

    @pl.when(step == 0)
    def _():
        stack_rows(act, (own, near, far, last))
        total[...] = jnp.zeros_like(total)

    dmixed = dot(act[...], w_out[...], COLS).astype(LOW)
    for h in range(w_out.shape[1] // DH):
        at = slice(h * DH, (h + 1) * DH)
        probs = probs_in[h]
        dm = dmixed[:, at]
        dqkv_out[2, :, at] = dot(probs.astype(LOW), dm, ROWS).astype(LOW)
        dprobs = dot(dm, qkv[2, :, at], BOTH)
        terms = jnp.sum(probs * dprobs, axis=-1, keepdims=True)
        ds = (probs * (dprobs - terms) * scale).astype(LOW)
        dqkv_out[0, :, at] = dot(ds, qkv[1, :, at], COLS).astype(LOW)
        dqkv_out[1, :, at] = dot(ds, qkv[0, :, at], ROWS).astype(LOW)
    part = dot(dqkv_out[0], w_qkv[0], BOTH)
    part += dot(dqkv_out[1], w_qkv[1], BOTH)
    part += dot(dqkv_out[2], w_qkv[2], BOTH)
    total[...] += part
    for row, t in enumerate((0, 2)):
        sum_out[row : row + 1] = jnp.sum(dqkv_out[t].astype(FULL), axis=0, keepdims=True)

    @pl.when(step == pl.num_programs(0) - 1)
    def _():
        keep_out[...] = total[:half]
        send_out[...] = total[half : half + half // 2].astype(LOW)
        give_rows(total[half + half // 2 :].astype(LOW), (fold_out, fold_last))


def attention_back(own, near, far, last, w_out, qkv, probs, w_qkv, group=2):
    d_model, width = w_out.shape
    rows = qkv.shape[1]
    cols = group * DH
    return pl.pallas_call(
        functools.partial(back_kernel, DH**-0.5),
        grid=(width // cols,),
        in_specs=[
            *[whole(own.shape)] * 4,
            pl.BlockSpec((d_model, cols), lambda i: (0, i)),
            pl.BlockSpec((3, rows, cols), lambda i: (0, 0, i)),
            pl.BlockSpec((group, rows, rows), lambda i: (i, 0, 0)),
            pl.BlockSpec((3, d_model, cols), lambda i: (0, 0, i)),
        ],
        out_specs=[
            pl.BlockSpec((3, rows, cols), lambda i: (0, 0, i)),
            pl.BlockSpec((2, cols), lambda i: (0, i)),
            whole((rows // 2, d_model)),
            whole((rows // 4, d_model)),
            *[whole((rows // 8, d_model))] * 2,
        ],
        out_shape=[
            shape_of((3, rows, width), LOW),
            shape_of((2, width), FULL),
            shape_of((rows // 2, d_model), FULL),
            shape_of((rows // 4, d_model), LOW),
            *[shape_of((rows // 8, d_model), LOW)] * 2,
        ],
        scratch_shapes=[pltpu.VMEM((rows, d_model), LOW), pltpu.VMEM((rows, d_model), FULL)],
        compiler_params=params(48),
        cost_estimate=cost(15),
    )(own, near, far, last, w_out, qkv, probs, w_qkv)


def leave_kernel(keep, got, last, x_own, dh, gain, down_keep, down_got, down_last, resid, biases, *outs):
    da1 = keep[...] + got[...].astype(FULL) + last[...].astype(FULL)
    unit, inverse = normalize(x_own[...].astype(FULL))
    grad = (dh[...] + norm_back(da1, unit, inverse, gain[...].astype(FULL))).astype(LOW)
    down = down_keep[...] + down_got[...].astype(FULL) + down_last[...].astype(FULL)
    output = (resid[...] + down + biases[1:].astype(FULL)).astype(LOW)
    sub = output.shape[0]
    for at, out in enumerate(outs[:-1]):

        @pl.when(pl.program_id(0) == at)
        def _(out=out):
            out[:sub, :] = output
            out[sub:, :] = grad

    add_rows(outs[-1], (da1 * unit, da1))


def leave(keep, got, last, x_own, dh, gain, down_keep, down_got, down_last, resid, biases, parts):
    dims = x_own.shape
    rows = dims[0] // parts
    block = pl.BlockSpec((rows, dims[1]), lambda i: (i, 0))
    piece = (2 * rows, dims[1])
    return pl.pallas_call(
        leave_kernel,
        grid=(parts,),
        in_specs=[block] * 5 + [whole(gain.shape)] + [block] * 4 + [whole(biases.shape)],
        out_specs=[whole(piece)] * parts + [whole((2, dims[1]))],
        out_shape=[shape_of(piece, LOW)] * parts + [shape_of((2, dims[1]), FULL)],
        compiler_params=params(16),
        cost_estimate=cost(3),
    )(keep, got, last, x_own, dh, gain, down_keep, down_got, down_last, resid, biases)


def place_kernel(items, sub, spot, own, near, far, last, output, grad):
    for at, source in enumerate((own, near, far, last)):
        for s in range(items):
            row = 2 * s * sub
            output[spot[s], spot[items + at]] = source[row : row + sub, :]
            grad[spot[s], spot[items + at]] = source[row + sub : row + 2 * sub, :].astype(FULL)


def place(own, near, far, last, spot, items, mp):
    rows, d_model = own.shape
    sub = rows // items // 2
    vmem = pl.BlockSpec(memory_space=pltpu.VMEM)
    dims = (items, mp, sub, d_model)
    output, grad = pl.pallas_call(
        functools.partial(place_kernel, items, sub),
        in_specs=[pl.BlockSpec(memory_space=pltpu.SMEM)] + [vmem] * 4,
        out_specs=[vmem, vmem],
        out_shape=[shape_of(dims, LOW), shape_of(dims, FULL)],
        compiler_params=params(24),
        cost_estimate=cost(6),
    )(spot, own, near, far, last)
    return output.reshape(items, mp * sub, d_model), grad.reshape(items, mp * sub, d_model)


def product_kernel(counts, blocks, added, spots, *refs):
    out = refs[-1]
    refs = list(refs[:-1])
    columns = []
    for _ in range(blocks):
        columns.append([])
        for count in counts:
            pieces = [refs.pop(0)[...] for _ in range(count)]
            columns[-1].append(pieces[0] if count == 1 else jnp.concatenate(pieces, axis=0))
    units = [refs.pop(0) for _ in counts]
    for at in range(blocks):
        part = sum(dot(c, u[0], ROWS) for c, u in zip(columns[at], units))
        rows = part.shape[0]
        here = slice(at * rows, (at + 1) * rows)
        if added:
            part = part + refs[0][0, here].astype(FULL)
        out[0, here] = part.astype(LOW)


def products(spots, sources, blocks, chunk, added=None, block=0, start=0, count=None):
    if count is None:
        start, count = 0, sources[0][2].shape[0]
    in_specs, args = [], []
    for k in blocks:
        for pieces, base, _ in sources:
            for piece in pieces:
                at = k + base
                in_specs.append(pl.BlockSpec((piece.shape[0], chunk), lambda i, spots, at=at: (0, spots[at])))
                args.append(piece)
    for _, _, unit in sources:
        in_specs.append(pl.BlockSpec((1, unit.shape[1], TILE), lambda i, spots: (start + i, 0, 0)))
        args.append(unit)
    size = chunk * len(blocks)
    if added is not None:
        in_specs.append(pl.BlockSpec((1, size, TILE), lambda i, spots: (i, block, 0)))
        args.append(added)
    counts = tuple(len(pieces) for pieces, _, _ in sources)
    return pl.pallas_call(
        functools.partial(product_kernel, counts, len(blocks), added is not None),
        grid_spec=pltpu.PrefetchScalarGridSpec(
            num_scalar_prefetch=1,
            grid=(count,),
            in_specs=in_specs,
            out_specs=pl.BlockSpec((1, size, TILE), lambda i, spots: (i, 0, 0)),
        ),
        out_shape=shape_of((count, size, TILE), LOW),
        compiler_params=params(24),
        cost_estimate=cost(0.6 * count * len(blocks)),
    )(spots, *args)


def pass_kernel(got, mine, out):
    out[...] = (mine[...].astype(FULL) + got[...].astype(FULL)).astype(LOW)


def pass_on(got, mine, rows, start, count):
    steps = mine.shape[0]
    part = pl.BlockSpec((1, rows, TILE), lambda i, j: (i, start + j, 0))
    return pl.pallas_call(
        pass_kernel,
        grid=(steps, count),
        in_specs=[part, part],
        out_specs=pl.BlockSpec((1, rows, TILE), lambda i, j: (i, j, 0)),
        out_shape=shape_of((steps, count * rows, TILE), LOW),
        compiler_params=params(16),
        cost_estimate=cost(steps),
    )(got, mine)


def finish_kernel(n_inner, n_end, inner, *refs):
    out = refs[-1]
    for flag, terms in ((1, refs[:n_inner]), (0, refs[n_inner : n_inner + n_end])):

        @pl.when(inner[0] == flag)
        def _(terms=terms):
            out[...] = sum(term[...].astype(FULL) for term in terms).reshape(out.shape)


def finish(last, inner, inner_terms, end_terms, first, total, split, before):
    steps, chunk, _ = last.shape
    head = pl.BlockSpec((1, chunk, TILE), lambda i: (i, 0, 0))
    args = [inner, *inner_terms, *end_terms, last]
    in_specs = [pl.BlockSpec(memory_space=pltpu.SMEM)] + [head] * (len(args) - 1)
    aliases = {}
    if before is not None:
        aliases = {len(args): 0}
        in_specs.append(pl.BlockSpec(memory_space=pl.ANY))
        args.append(before)
    if split:
        out_spec = pl.BlockSpec((1, chunk, TILE), lambda i: (first + i, 0, 0))
        out_shape = shape_of((total, chunk, TILE), FULL)
    else:
        out_spec = pl.BlockSpec((chunk, TILE), lambda i: (0, first + i))
        out_shape = shape_of((chunk, total * TILE), FULL)
    return pl.pallas_call(
        functools.partial(finish_kernel, len(inner_terms), len(end_terms) + 1),
        grid=(steps,),
        in_specs=in_specs,
        out_specs=out_spec,
        out_shape=out_shape,
        input_output_aliases=aliases,
        compiler_params=params(16),
        cost_estimate=cost(steps),
    )(*args)


def join_kernel(*refs):
    stack_rows(refs[-1], refs[:-1])


def joined(first, *others):
    rows = first.shape[0] + sum(p.shape[0] for p in others)
    return pl.pallas_call(
        join_kernel,
        out_shape=shape_of((rows, first.shape[1]), LOW),
        compiler_params=params(16),
        cost_estimate=cost(1),
    )(first, *others)


class Names:
    def __getattr__(self, name):
        return name


N = Names()
PLAN = (
    (
        N.begin,
        (),
        ((N.y_act_one,), (N.c_act_one,)),
    ),
    (
        N.dy,
        (),
        ((N.d_act_one,), (N.y_dy, N.y_act_one), (N.c_dy,)),
    ),
    (
        N.attend,
        (),
        ((N.k_attn,), (N.l_attn,), (N.n_attn,), (N.x_mixed,), (N.d_dy,)),
    ),
    (
        N.fold_attn,
        (N.y_dy,),
        ((N.y_attn,), (N.e_dy,)),
    ),
    (
        N.norm_two,
        (N.x_mixed,),
        ((N.y_act_two,), (N.c_act_two,), (N.d_act_two,), (N.x_halves,)),
    ),
    (
        N.feed_one,
        (N.e_dy,),
        ((N.x_u0,), (N.e_g0,), (N.y_halves,), (N.c_halves,)),
    ),
    (
        N.feed_two,
        (),
        ((N.k_da2,), (N.l_da2,), (N.n_da2,), (N.d_e_dy,)),
    ),
    (
        N.down,
        (),
        ((N.k_down,), (N.l_down,), (N.n_down,)),
    ),
    (
        N.fold_da2,
        (N.y_halves, N.k_attn),
        ((N.y_da2,), (N.d_halves,)),
    ),
    (
        N.cross_g0,
        (),
        ((N.m_g0,), (N.e_g1, N.e_g0)),
    ),
    (
        N.norm_back_two,
        (),
        ((N.y_dattn,), (N.c_dattn,), (N.d_dattn,), (N.x_u1,)),
    ),
    (
        N.start_u0,
        (),
        (),
    ),
    (
        N.cross_g1,
        (),
        ((N.m_g1, N.m_g0), (N.e_u0,)),
    ),
    (
        N.attend_back,
        (),
        ((N.k_da1,), (N.l_da1,), (N.n_da1,), (N.x_last, N.x_u1)),
    ),
    (
        N.start_u1,
        (),
        (),
    ),
    (
        N.fold_da1,
        (),
        ((N.y_da1, N.y_act_two), (N.x_q, N.x_last)),
    ),
    (
        N.fold_down,
        (),
        ((N.y_down, N.y_da1), (N.y_last, N.y_down)),
    ),
    (
        N.sum_up_g0,
        (),
        (),
    ),
    (
        N.cross_u0,
        (N.x_last,),
        ((N.m_u0, N.m_g1), (N.e_u1,)),
    ),
    (
        N.norm_back_one,
        (),
        ((N.sum_tokens,), (N.c_last,), (N.d_last,)),
    ),
    (
        N.start_q0,
        (),
        ((N.x_g0,),),
    ),
    (
        N.start_o0,
        (),
        (),
    ),
    (
        N.start_q1,
        (),
        (),
    ),
    (
        N.cross_u1,
        (N.e_u1,),
        ((N.e_o0,),),
    ),
    (
        N.sum_up_g1,
        (),
        ((N.x_g1, N.x_g0),),
    ),
    (
        N.back_g0,
        (),
        ((N.o_g0,),),
    ),
    (
        N.cross_o0,
        (),
        ((N.e_q0,), (N.m_o0, N.m_u1), (N.m_u1, N.m_u0)),
    ),
    (
        N.back_u0,
        (),
        (),
    ),
    (
        N.back_g1,
        (),
        ((N.o_g1, N.o_u0), (N.o_u0, N.o_g0)),
    ),
    (
        N.end_u0,
        (),
        (),
    ),
    (
        N.back_u1,
        (),
        ((N.o_u1, N.o_g1),),
    ),
    (
        N.cross_q0,
        (),
        ((N.ends,), (N.m_q0, N.m_o0)),
    ),
    (
        N.end_g1,
        (),
        (),
    ),
    (
        N.end_g0,
        (),
        (),
    ),
    (
        N.ends_join,
        (),
        ((N.y_ends,), (N.c_ends,), (N.e_q1,)),
    ),
    (
        N.back_o0,
        (),
        ((N.o_o0, N.o_u1),),
    ),
    (
        N.end_u1,
        (),
        (),
    ),
    (
        N.end_o0,
        (),
        (),
    ),
    (
        N.cross_q1,
        (),
        ((N.sum_dp,), (N.m_q1,), (N.sum_one,), (N.d_ends,)),
    ),
    (
        N.back_q0,
        (),
        ((N.o_q0,),),
    ),
    (
        N.back_q1,
        (),
        ((N.o_q1,),),
    ),
    (
        N.end_q0,
        (),
        ((N.sum_two,),),
    ),
    (
        N.ends_place,
        (),
        (),
    ),
    (
        N.end_q1,
        (),
        (),
    ),
)
PLAIN = (
    N.begin,
    N.dy,
    N.attend,
    N.fold_attn,
    N.norm_two,
    N.feed_one,
    N.feed_two,
    N.down,
    N.fold_da2,
    N.norm_back_two,
    N.attend_back,
    N.fold_da1,
    N.fold_down,
    N.norm_back_one,
    N.ends_join,
    N.ends_place,
)
PLAIN_SENDS = (
    N.y_act_one,
    N.c_act_one,
    N.d_act_one,
    N.y_dy,
    N.c_dy,
    N.k_attn,
    N.l_attn,
    N.n_attn,
    N.d_dy,
    N.y_attn,
    N.y_act_two,
    N.c_act_two,
    N.d_act_two,
    N.k_da2,
    N.l_da2,
    N.n_da2,
    N.k_down,
    N.l_down,
    N.n_down,
    N.y_da2,
    N.y_dattn,
    N.c_dattn,
    N.d_dattn,
    N.k_da1,
    N.l_da1,
    N.n_da1,
    N.y_da1,
    N.y_down,
    N.sum_tokens,
    N.ends,
    N.y_ends,
    N.c_ends,
    N.sum_dp,
    N.sum_one,
    N.d_ends,
    N.sum_two,
)


def on_device(
    dp,
    blk,
    mp,
    inputs,
    lengths,
    w_qkv,
    b_qv,
    w_out,
    out_biases,
    ln_gains,
    ln_shifts,
    w_up,
    b_up,
    w_down,
    cotangent,
):
    items, block_len, d_model = inputs.shape
    width = w_qkv.shape[2]
    sub = block_len // mp
    own_rows = blk * sub
    rows = own_rows * mp
    chunk = d_model // (dp * blk)
    half_cols = blk * chunk
    paired = dp == 2
    order = Order()
    x, z, me = lax.axis_index("dp"), lax.axis_index("blk"), lax.axis_index("mp")

    def swap_core(array):
        return lax.ppermute(array, "mp", flip(mp, 1))

    def swap_y(array):
        return lax.ppermute(array, "mp", flip(mp, 2))

    def swap_dp(array):
        return lax.ppermute(array, "dp", flip(dp, 1))

    def along(array, pairs):
        return lax.ppermute(array, "blk", pairs)

    def to_items(array, *ties):
        mine = lax.dynamic_slice_in_dim(array, me * sub, sub, axis=1)
        parts = {0: lax.dynamic_index_in_dim(mine, z, 0, keepdims=False)}
        for s in (1, blk - 1, 2):
            piece = lax.dynamic_index_in_dim(mine, lax.rem(z + s, blk), 0, keepdims=False)
            if ties:
                piece = after(piece, *ties)
            parts[s] = along(piece, shift(blk, s))
        return [parts[s] for s in range(blk)]

    spot = jnp.stack(
        [lax.rem(z + s, blk) for s in range(blk)] + [me ^ j for j in (0, 2, 1, 3)]
    ).astype(jnp.int32)
    in_block = jnp.arange(sub, dtype=jnp.int32)
    block_of = lax.rem(z - jnp.arange(blk, dtype=jnp.int32) + blk, blk)

    def positions_of(q):
        return (block_of[:, None] * block_len + q * sub + in_block[None, :]).reshape(-1)

    pos = jnp.concatenate([positions_of(me ^ j) for j in (0, 2, 1, 3)])
    length = lax.dynamic_slice_in_dim(lengths, z, 1)

    def other_half(array):
        return lax.dynamic_slice_in_dim(array, (1 - x) * half_cols, half_cols, axis=1)

    line = [jnp.where(z < blk // 2, k, blk - 1 - k) for k in range(blk)]
    inner = jnp.where((z == 0) | (z == blk - 1), 0, 1).astype(jnp.int32)[None]
    MINE, HALF, SECOND, THEIRS = (blk * i for i in range(4))
    spots = jnp.stack(
        [x * blk + at for at in line]
        + line
        + [blk + at for at in line]
        + [(1 - x) * blk + at for at in line]
    ).astype(jnp.int32)
    to_inner, across, to_end = [(0, 1), (3, 2)], [(1, 2), (2, 1)], [(1, 0), (2, 3)]

    def grad_plain(full, unit):
        part = jnp.einsum("rd,trc->dtc", jnp.concatenate(full), unit, preferred_element_type=FULL)
        part = lax.psum_scatter(part.astype(LOW), ("dp", "blk"), scatter_dimension=0, tiled=True)
        return part.astype(FULL)

    w_three = w_qkv.transpose(1, 0, 2)
    b_three = jnp.stack([b_qv[0], jnp.zeros_like(b_qv[0]), b_qv[1]]).astype(FULL)
    gain_one, gain_two = ln_gains[:1], ln_gains[1:]
    shift_one, shift_two = ln_shifts[:1], ln_shifts[1:]
    tiles = w_up.shape[1] // TILE
    some = tiles // 2
    b_row = b_up[None]
    v = {}
    steps = {}
    sends = {}

    def step(function):
        steps[function.__name__] = function
        return function

    def send(name, swap, *operand):
        def run(needs):
            value = operand[0]() if callable(operand[0]) else v[operand[0]]
            ties = [v[need] for need in (*operand[1:], *needs)]
            v[name] = swap(after(value, order.last, *jax.tree.leaves(ties)))

        sends[name] = run

    def cut(array, parts):
        rows = array.shape[0] // parts
        return [array[i * rows : (i + 1) * rows] for i in range(parts)]

    def gather(name, own):
        send(N.y_ + name, swap_y, own)
        send(N.c_ + name, swap_core, own)
        send(N.d_ + name, swap_core, N.y_ + name)

    def gathered(name, own):
        return [v[own], v[N.y_ + name], v[N.c_ + name], v[N.d_ + name]]

    def scatter(name):
        send(N.k_ + name, swap_core, N.t_ + name)
        send(N.l_ + name, swap_core, N.u_ + name)
        send(N.n_ + name, swap_core, N.w_ + name)
        send(N.y_ + name, swap_y, N.f_ + name)

        def fold_it():
            v[N.f_ + name] = order.run(
                fold, v[N.l_ + name], v[N.n_ + name], v[N.keep_ + name]
            )

        steps[N.fold_ + name] = fold_it

    def scattered(name):
        return [v[N.keep_ + name], v[N.k_ + name], v[N.y_ + name]]

    def terms_of(name, terms):
        v[N.keep_ + name], v[N.t_ + name], v[N.u_ + name], v[N.w_ + name] = terms

    x_parts = to_items(inputs)
    dy_parts = to_items(cotangent, *x_parts[1:])
    gather(N.act_one, N.act_one_own)
    gather(N.dy, N.dy_own)
    gather(N.act_two, N.act_two_own)
    gather(N.dattn, N.dattn_own)
    for name in (N.attn, N.da2, N.down, N.da1):
        scatter(name)

    @step
    def begin():
        v[N.x_own], v[N.act_one_own] = enter(x_parts[0], gain_one, shift_one, *x_parts[1:])
        order.last = v[N.act_one_own]

    @step
    def dy():
        v[N.dy_own] = order.run(masked, dy_parts[0], length, pos[:own_rows, None], *dy_parts[1:])

    @step
    def attend():
        own, *others = gathered(N.act_one, N.act_one_own)
        v[N.qkv], v[N.probs], v[N.mixed], *terms = order.run(
            attention, own, *others, w_three, b_three, w_out, pos, length
        )
        terms_of(N.attn, terms)

    send(N.x_mixed, swap_dp, N.mixed)
    send(
        N.e_dy,
        lambda array: along(array, to_inner),
        lambda: jnp.concatenate([v[N.dy_own], v[N.y_dy]], axis=0),
    )
    send(N.d_e_dy, swap_core, N.e_dy)

    @step
    def norm_two():
        keep, got, last = scattered(N.attn)
        v[N.resid], v[N.act_two_own] = order.run(
            middle, v[N.x_own], keep, got, last, out_biases, gain_two, shift_two
        )

    send(
        N.x_halves,
        swap_dp,
        lambda: jnp.concatenate(
            [other_half(v[name]) for name in (N.act_one_own, N.act_two_own)], axis=1
        ),
    )
    gather(N.halves, N.x_halves)

    def feed_half(before, first):
        own, *others = gathered(N.act_two, N.act_two_own)
        dy = gathered(N.dy, N.dy_own)
        return order.run(feed, own, *others, dy, w_up, b_row, w_down, before, first, some)

    @step
    def feed_one():
        v[N.gel_a], v[N.dup_a], v[N.up_sum_a], v[N.before] = feed_half(None, 0)

    @step
    def feed_two():
        v[N.gel_b], v[N.dup_b], v[N.up_sum_b], *terms = feed_half(v[N.before], some)
        terms_of(N.da2, terms)

    send(N.x_u0, swap_dp, N.dup_a)
    send(N.x_u1, swap_dp, N.dup_b)

    @step
    def down():
        terms_of(N.down, order.run(down_part, v[N.gel_a], v[N.gel_b], w_down))

    @step
    def norm_back_two():
        keep, got, last = scattered(N.da2)
        v[N.dh], v[N.dattn_own], v[N.sums_two] = order.run(
            turn, keep, got, last, v[N.resid], v[N.dy_own], gain_two
        )

    send(N.x_last, swap_dp, lambda: other_half(v[N.dattn_own]))
    gather(N.last, N.x_last)

    @step
    def attend_back():
        own, *others = gathered(N.dattn, N.dattn_own)
        v[N.dqkv], v[N.qkv_sum], *terms = order.run(
            attention_back, own, *others, w_out, v[N.qkv], v[N.probs], w_three
        )
        terms_of(N.da1, terms)

    send(N.x_q, swap_dp, N.dqkv)

    @step
    def norm_back_one():
        *v[N.ends_parts], v[N.sums_one] = order.run(
            leave,
            *scattered(N.da1),
            v[N.x_own],
            v[N.dh],
            gain_one,
            *scattered(N.down),
            v[N.resid],
            out_biases,
            blk,
        )

    def move_ends(parts):
        return [parts[0]] + [along(parts[s], shift(blk, -s)) for s in range(1, blk)]

    def ends(needs):
        tie = [order.last, *[v[n] for n in needs]]
        v[N.ends] = move_ends([after(part, *tie) for part in v[N.ends_parts]])

    sends[N.ends] = ends

    def sum_tokens(needs):
        tie = [order.last, *[v[n] for n in needs]]
        sums = jnp.concatenate([v[N.sums_one], v[N.sums_two]], axis=0).reshape(-1)
        sums = after(sums, *tie)
        sums = sums + swap_core(sums)
        sums = sums + swap_y(sums)
        rest = [v[name].reshape(-1) for name in (N.qkv_sum, N.up_sum_a, N.up_sum_b)]
        v[N.sums] = jnp.concatenate([sums, *rest])

    def sum_dp(needs):
        sums = after(v[N.sums], order.last, *[v[n] for n in needs])
        bit = 1
        while bit < dp:
            sums = sums + lax.ppermute(sums, "dp", flip(dp, bit))
            bit *= 2
        v[N.sums] = sums

    def sum_step(bit):
        def run(needs):
            sums = after(v[N.sums], order.last, *[v[n] for n in needs])
            v[N.sums] = sums + along(sums, flip(blk, bit))

        return run

    sends[N.sum_tokens] = sum_tokens
    sends[N.sum_one] = sum_step(1)
    sends[N.sum_two] = sum_step(2)
    sends[N.sum_dp] = sum_dp

    @step
    def ends_join():
        v[N.ends_own] = order.run(joined, *v[N.ends])

    gather(N.ends, N.ends_own)

    @step
    def ends_place():
        v[N.output], v[N.input_grad] = order.run(
            place, *gathered(N.ends, N.ends_own), spot, items, mp
        )

    def token_piece(name, first, unit):
        def sources():
            ends = [v[N.e_dy], v[N.d_e_dy]]
            return [(gathered(N.dy, N.dy_own), MINE, v[unit]), (ends, MINE, v[N.e_ + name])]

        def cross():
            blocks = (2, 3, 2 + THEIRS, 3 + THEIRS)
            v[N.cross_ + name] = order.run(products, spots, sources(), blocks, chunk)

        def sum_up():
            blocks = (1, 0, 1 + THEIRS, THEIRS)
            v[N.all_ + name] = order.run(
                products, spots, sources(), blocks, chunk, v[N.m_ + name]
            )

        def back():
            v[N.back_ + name] = order.run(
                pass_on, v[N.x_ + name], v[N.all_ + name], chunk, 1, 1
            )

        def end():
            terms = [v[N.all_ + name], v[N.x_ + name]]
            v[N.grad_down] = order.run(
                finish, v[N.o_ + name], inner, terms, [], first, tiles, False, v.get(N.grad_down)
            )

        for function in (cross, sum_up, back, end):
            steps[function.__name__ + N._ + name] = function
        send(N.e_ + name, lambda array: along(array, to_inner), unit)
        send(N.m_ + name, lambda array: along(array, across), N.cross_ + name)
        send(N.x_ + name, swap_dp, lambda: v[N.all_ + name][:, 2 * chunk :])
        send(N.o_ + name, lambda array: along(array, to_end), N.back_ + name)

    def sum_piece(name, columns, units, target, first, total, split, count=None):
        def sources():
            return [(c(), base, u) for (c, base), u in zip(columns, units())]

        def start():
            v[N.mine_ + name] = order.run(
                products, spots, sources(), (1, 2, 3), chunk, None, 0, first, count
            )

        def cross():
            v[N.cross_ + name] = order.run(
                pass_on, v[N.e_ + name], v[N.mine_ + name], chunk, 1, 2
            )

        def back():
            v[N.back_ + name] = order.run(
                products, spots, sources(), (0,), chunk, v[N.m_ + name], 1, first, count
            )

        def end():
            terms = [v[N.mine_ + name], v[N.e_ + name], v[N.m_ + name]]
            v[target] = order.run(
                finish, v[N.o_ + name], inner, terms, [v[N.back_ + name]], first, total, split, v.get(target)
            )

        for function in (start, cross, back, end):
            steps[function.__name__ + N._ + name] = function
        send(N.e_ + name, lambda array: along(array, to_inner), N.mine_ + name)
        send(N.m_ + name, lambda array: along(array, across), N.cross_ + name)
        send(N.o_ + name, lambda array: along(array, to_end), N.back_ + name)

    def columns_of(name, own):
        return lambda: gathered(name, own)

    act_one, act_two, dattn, halves, last = (
        columns_of(name, own)
        for name, own in (
            (N.act_one, N.act_one_own),
            (N.act_two, N.act_two_own),
            (N.dattn, N.dattn_own),
            (N.halves, N.x_halves),
            (N.last, N.x_last),
        )
    )
    token_piece(N.g0, 0, N.gel_a)
    token_piece(N.g1, some, N.gel_b)
    both = [(act_two, MINE), (halves, SECOND)]
    sum_piece(N.u0, both, lambda: [v[N.dup_a], v[N.x_u0]], N.grad_up, 0, tiles, False)
    sum_piece(N.u1, both, lambda: [v[N.dup_b], v[N.x_u1]], N.grad_up, some, tiles, False)
    both = [(act_one, MINE), (halves, HALF)]
    sum_piece(N.q0, both, lambda: [v[N.dqkv], v[N.x_q]], N.grad_qkv, 0, 3, True, 2)
    sum_piece(N.q1, both, lambda: [v[N.dqkv], v[N.x_q]], N.grad_qkv, 2, 3, True, 1)
    both = [(dattn, MINE), (last, HALF)]
    sum_piece(N.o0, both, lambda: [v[N.mixed][None], v[N.x_mixed][None]], N.grad_out, 0, 1, False)

    for name, needs, starts in PLAN:
        if paired or name in PLAIN:
            order.needs = [leaf for need in needs if need in v for leaf in jax.tree.leaves(v[need])]
            with jax.named_scope(name):
                steps[name]()
        for entry in starts:
            transfer, *ties = entry
            if paired or transfer in PLAIN_SENDS:
                with jax.named_scope(transfer):
                    sends[transfer]([tie for tie in ties if tie in v])
    if paired:
        grad_qkv = v[N.grad_qkv].transpose(1, 0, 2)
    else:
        gel = jnp.concatenate([v[N.gel_a], v[N.gel_b]], axis=0)
        dup = jnp.concatenate([v[N.dup_a], v[N.dup_b]], axis=0)
        v[N.grad_down] = grad_plain(gathered(N.dy, N.dy_own), gel).reshape(chunk, -1)
        v[N.grad_up] = grad_plain(act_two(), dup).reshape(chunk, -1)
        v[N.grad_out] = grad_plain(dattn(), v[N.mixed][None]).reshape(chunk, -1)
        grad_qkv = grad_plain(act_one(), v[N.dqkv])

    sums = v[N.sums]
    per_token = sums[: 6 * d_model].reshape(6, d_model)
    grad_qv_bias = sums[6 * d_model : 6 * d_model + 2 * width].reshape(2, width)
    return (
        v[N.output],
        v[N.input_grad],
        grad_qkv,
        grad_qv_bias,
        v[N.grad_out],
        per_token[4:6],
        jnp.stack([per_token[0], per_token[2]]),
        jnp.stack([per_token[1], per_token[3]]),
        v[N.grad_up],
        sums[6 * d_model + 2 * width :],
        v[N.grad_down],
    )


def solution(mesh):
    sizes = [mesh.shape[name] for name in ("dp", "blk", "mp")]
    in_specs = (
        P("dp", "blk", None),
        P("dp"),
        P(None, None, "mp"),
        P(None, "mp"),
        P(None, "mp"),
        P(),
        P(),
        P(),
        P(None, "mp"),
        P("mp"),
        P(None, "mp"),
        P("dp", "blk", None),
    )
    out_specs = (
        P("dp", "blk", None),
        P("dp", "blk", None),
        P(("dp", "blk"), None, "mp"),
        P(None, "mp"),
        P(("dp", "blk"), "mp"),
        P(),
        P(),
        P(),
        P(("dp", "blk"), "mp"),
        P("mp"),
        P(("dp", "blk"), "mp"),
    )

    def step(*arrays):
        return on_device(*sizes, *arrays)

    return jax.shard_map(
        step, mesh=mesh, in_specs=in_specs, out_specs=out_specs, check_vma=False
    )
```

```python
import functools

import jax
import jax.numpy as jnp
from jax import lax
from jax.experimental import pallas as pl
from jax.experimental.pallas import tpu as pltpu
from jax.sharding import PartitionSpec as P

DH = 128
LOW = jnp.bfloat16
FULL = jnp.float32
TILE = 512
BAND = 32


def flip(size, bit):
    return [(i, i ^ bit) for i in range(size)]


def shift(size, step):
    return [(i, (i + step) % size) for i in range(size)]


def after(value, *others):
    return lax.optimization_barrier((value, *others))[0]


class Order:
    def __init__(self):
        self.last = None
        self.needs = ()

    def run(self, function, first, *others):
        waits = list(self.needs) + ([] if self.last is None else [self.last])
        if waits:
            first = after(first, *waits)
        results = function(first, *others)
        self.last = results[-1] if isinstance(results, (list, tuple)) else results
        self.needs = ()
        return results


def dot(left, right, dims):
    return lax.dot_general(left, right, (dims, ((), ())), preferred_element_type=FULL)


COLS = ((1,), (0,))
BOTH = ((1,), (1,))
ROWS = ((0,), (0,))


def shape_of(dims, kind):
    return jax.ShapeDtypeStruct(dims, kind)


def whole(dims):
    return pl.BlockSpec(dims, lambda *_: (0,) * len(dims))


def params(megabytes):
    return pltpu.CompilerParams(vmem_limit_bytes=megabytes << 20)


def cost(microseconds, share=0.05):
    flops = int(microseconds * share * 1153.5e6)
    return pl.CostEstimate(flops=flops, bytes_accessed=1, transcendentals=0)


def give_rows(values, targets):
    at = 0
    for target in targets:
        target[...] = values[at : at + target.shape[0]]
        at += target.shape[0]


def stack_rows(target, pieces):
    at = 0
    for piece in pieces:
        target[at : at + piece.shape[0], :] = piece[...]
        at += piece.shape[0]


def normalize(values):
    centered = values - jnp.mean(values, axis=-1, keepdims=True)
    variance = jnp.mean(centered * centered, axis=-1, keepdims=True)
    inverse = lax.rsqrt(variance + 1e-05)
    return centered * inverse, inverse


def norm_back(grad_norm, unit, inverse, gain):
    scaled = grad_norm * gain
    first = jnp.mean(scaled, axis=-1, keepdims=True)
    second = jnp.mean(scaled * unit, axis=-1, keepdims=True)
    return inverse * (scaled - first - unit * second)


def enter_kernel(first, gain, bias, *refs):
    pieces, (x_out, act_out) = (first, *refs[:-2]), refs[-2:]
    stack_rows(x_out, pieces)
    unit, _ = normalize(x_out[...].astype(FULL))
    act_out[...] = (unit * gain[...].astype(FULL) + bias[...].astype(FULL)).astype(LOW)


def enter(first, gain, bias, *others):
    rows, d_model = (1 + len(others)) * first.shape[0], first.shape[1]
    return pl.pallas_call(
        enter_kernel,
        out_shape=[shape_of((rows, d_model), LOW)] * 2,
        compiler_params=params(12),
        cost_estimate=cost(2),
    )(first, gain, bias, *others)


def mask_kernel(first, length, pos, *refs):
    pieces, out = (first, *refs[:-1]), refs[-1]
    stack_rows(out, pieces)
    out[...] = out[...] * (pos[...] < length[0]).astype(LOW)


def masked(first, length, pos, *others):
    rows, d_model = (1 + len(others)) * first.shape[0], first.shape[1]
    vmem = pl.BlockSpec(memory_space=pltpu.VMEM)
    return pl.pallas_call(
        mask_kernel,
        in_specs=[vmem, pl.BlockSpec(memory_space=pltpu.SMEM)] + [vmem] * (1 + len(others)),
        out_shape=shape_of((rows, d_model), LOW),
        compiler_params=params(12),
        cost_estimate=cost(1),
    )(first, length, pos, *others)


def attention_kernel(scale, own, near, far, last, w_qkv, b_qkv, w_out, pos_row, pos_col, length, qkv_out, probs_out, mixed_out, keep_out, send_out, fold_out, fold_last, act, bias, total):
    step = pl.program_id(0)
    half = act.shape[0] // 2

    @pl.when(step == 0)
    def _():
        stack_rows(act, (own, near, far, last))
        allowed = (pos_row[...] <= pos_col[...]) & (pos_row[...] < length[0])
        bias[...] = jnp.where(allowed, 0.0, -1e30)
        total[...] = jnp.zeros_like(total)

    for t in range(3):
        qkv_out[t] = (dot(act[...], w_qkv[t], COLS) + b_qkv[t][None]).astype(LOW)
    for h in range(w_out.shape[1] // DH):
        at = slice(h * DH, (h + 1) * DH)
        scores = dot(qkv_out[0, :, at], qkv_out[1, :, at], BOTH) * scale + bias[...]
        expo = jnp.exp(scores - jnp.max(scores, axis=-1, keepdims=True))
        probs = expo * (1.0 / jnp.sum(expo, axis=-1, keepdims=True))
        probs_out[h] = probs
        mixed_out[:, at] = dot(probs.astype(LOW), qkv_out[2, :, at], COLS).astype(LOW)
    total[...] += dot(mixed_out[...], w_out[...], BOTH)

    @pl.when(step == pl.num_programs(0) - 1)
    def _():
        keep_out[...] = total[:half]
        send_out[...] = total[half : half + half // 2].astype(LOW)
        give_rows(total[half + half // 2 :].astype(LOW), (fold_out, fold_last))


def attention(own, near, far, last, w_qkv, b_qkv, w_out, pos, length, group=2):
    d_model, width = w_out.shape
    rows = 4 * own.shape[0]
    cols = group * DH
    heads = width // DH
    return pl.pallas_call(
        functools.partial(attention_kernel, DH**-0.5),
        grid=(width // cols,),
        in_specs=[
            *[whole(own.shape)] * 4,
            pl.BlockSpec((3, d_model, cols), lambda i: (0, 0, i)),
            pl.BlockSpec((3, cols), lambda i: (0, i)),
            pl.BlockSpec((d_model, cols), lambda i: (0, i)),
            whole((1, rows)),
            whole((rows, 1)),
            pl.BlockSpec(memory_space=pltpu.SMEM),
        ],
        out_specs=[
            pl.BlockSpec((3, rows, cols), lambda i: (0, 0, i)),
            pl.BlockSpec((group, rows, rows), lambda i: (i, 0, 0)),
            pl.BlockSpec((rows, cols), lambda i: (0, i)),
            whole((rows // 2, d_model)),
            whole((rows // 4, d_model)),
            *[whole((rows // 8, d_model))] * 2,
        ],
        out_shape=[
            shape_of((3, rows, width), LOW),
            shape_of((heads, rows, rows), FULL),
            shape_of((rows, width), LOW),
            shape_of((rows // 2, d_model), FULL),
            shape_of((rows // 4, d_model), LOW),
            *[shape_of((rows // 8, d_model), LOW)] * 2,
        ],
        scratch_shapes=[
            pltpu.VMEM((rows, d_model), LOW),
            pltpu.VMEM((rows, rows), FULL),
            pltpu.VMEM((rows, d_model), FULL),
        ],
        compiler_params=params(48),
        cost_estimate=cost(14),
    )(own, near, far, last, w_qkv, b_qkv, w_out, pos[None, :], pos[:, None], length)


def fold_kernel(got, last, keep, out):
    half = got.shape[0]
    out[:half] = (keep[:half] + got[...].astype(FULL)).astype(LOW)
    out[half:] = (keep[half:] + last[...].astype(FULL)).astype(LOW)


def fold(got, last, keep):
    rows, d_model = 2 * got.shape[0], got.shape[1]
    return pl.pallas_call(
        fold_kernel,
        grid=(1,),
        in_specs=[whole(got.shape)] * 2 + [pl.BlockSpec((rows, d_model), lambda i: (1, 0))],
        out_specs=whole((rows, d_model)),
        out_shape=shape_of((rows, d_model), LOW),
        compiler_params=params(12),
        cost_estimate=cost(1),
    )(got, last, keep)


def middle_kernel(x_own, keep, got, last, biases, gain, bias, resid_out, act_out):
    attn = keep[...] + got[...].astype(FULL) + last[...].astype(FULL) + biases[:1].astype(FULL)
    resid = x_own[...].astype(FULL) + attn
    resid_out[...] = resid
    unit, _ = normalize(resid)
    act_out[...] = (unit * gain[...].astype(FULL) + bias[...].astype(FULL)).astype(LOW)


def middle(x_own, keep, got, last, biases, gain, bias):
    dims = x_own.shape
    block = pl.BlockSpec((BAND, dims[1]), lambda i: (i, 0))
    return pl.pallas_call(
        middle_kernel,
        grid=(dims[0] // BAND,),
        in_specs=[block] * 4 + [whole(biases.shape), whole(gain.shape), whole(bias.shape)],
        out_specs=[block] * 2,
        out_shape=[shape_of(dims, FULL), shape_of(dims, LOW)],
        compiler_params=params(12),
        cost_estimate=cost(2),
    )(x_own, keep, got, last, biases, gain, bias)


def feed_kernel(closing, own, near, far, last, dy_own, dy_near, dy_far, dy_last, w_up, b_up, w_down, *rest):
    gel_out, dup_out, sum_out = rest[closing : closing + 3]
    act, dy, total = rest[-3:]
    step = pl.program_id(0)
    half = act.shape[0] // 2

    @pl.when(step == 0)
    def _():
        stack_rows(act, (own, near, far, last))
        stack_rows(dy, (dy_own, dy_near, dy_far, dy_last))
        total[...] = rest[0][...] if closing else jnp.zeros_like(total)

    upper = dot(act[...], w_up[...], COLS) + b_up[...].astype(FULL)
    dgel = dot(dy[...], w_down[...], COLS)
    phi = 0.5 + 0.5 * lax.erf(upper * (0.5**0.5))
    gel_out[0] = (upper * phi).astype(LOW)
    slope = phi + upper * jnp.exp(-0.5 * upper * upper) * 0.3989422804014327
    dup = (dgel * slope).astype(LOW)
    dup_out[0] = dup
    sum_out[...] = jnp.sum(dup.astype(FULL), axis=0, keepdims=True)
    total[...] += dot(dup, w_up[...], BOTH)

    @pl.when(step == pl.num_programs(0) - 1)
    def _():
        if closing:
            keep_out, send_out, fold_out, fold_last = rest[4:8]
            keep_out[...] = total[:half]
            send_out[...] = total[half : half + half // 2].astype(LOW)
            give_rows(total[half + half // 2 :].astype(LOW), (fold_out, fold_last))
        else:
            rest[3][...] = total[...]


def feed(own, near, far, last, dy, w_up, b_up, w_down, before, first, steps):
    d_model = own.shape[1]
    rows = 4 * own.shape[0]
    closing = before is not None
    out_specs = [pl.BlockSpec((1, rows, TILE), lambda i: (i, 0, 0))] * 2
    out_specs.append(pl.BlockSpec((1, TILE), lambda i: (0, i)))
    out_shape = [shape_of((steps, rows, TILE), LOW)] * 2 + [shape_of((1, steps * TILE), FULL)]
    if closing:
        ends = [((rows // 2, d_model), FULL)]
        ends += [((rows // at, d_model), LOW) for at in (4, 8, 8)]
    else:
        ends = [((rows, d_model), FULL)]
    return pl.pallas_call(
        functools.partial(feed_kernel, int(closing)),
        grid=(steps,),
        in_specs=[
            *[whole(own.shape)] * 8,
            pl.BlockSpec((d_model, TILE), lambda i: (0, first + i)),
            pl.BlockSpec((1, TILE), lambda i: (0, first + i)),
            pl.BlockSpec((d_model, TILE), lambda i: (0, first + i)),
        ]
        + [whole((rows, d_model))] * closing,
        out_specs=out_specs + [whole(dims) for dims, _ in ends],
        out_shape=out_shape + [shape_of(*end) for end in ends],
        scratch_shapes=[
            pltpu.VMEM((rows, d_model), LOW),
            pltpu.VMEM((rows, d_model), LOW),
            pltpu.VMEM((rows, d_model), FULL),
        ],
        compiler_params=params(58),
        cost_estimate=cost(11, 1.0 if closing else 0.5),
    )(own, near, far, last, *dy, w_up, b_up, w_down, *([before] if closing else []))


def down_kernel(gel_first, gel_rest, w_down, keep_out, send_out, fold_out, fold_last, total):
    step = pl.program_id(0)
    half = total.shape[0] // 2

    @pl.when(step == 0)
    def _():
        total[...] = jnp.zeros_like(total)

    @pl.when(step < pl.num_programs(0) // 2)
    def _():
        total[...] += dot(gel_first[0], w_down[...], BOTH)

    @pl.when(step >= pl.num_programs(0) // 2)
    def _():
        total[...] += dot(gel_rest[0], w_down[...], BOTH)

    @pl.when(step == pl.num_programs(0) - 1)
    def _():
        keep_out[...] = total[:half]
        send_out[...] = total[half : half + half // 2].astype(LOW)
        give_rows(total[half + half // 2 :].astype(LOW), (fold_out, fold_last))


def down_part(gel_first, gel_rest, w_down):
    d_model, units = w_down.shape
    rows = gel_first.shape[1]
    half = units // TILE // 2
    return pl.pallas_call(
        down_kernel,
        grid=(units // TILE,),
        in_specs=[
            pl.BlockSpec((1, rows, TILE), lambda i: (jnp.minimum(i, half - 1), 0, 0)),
            pl.BlockSpec((1, rows, TILE), lambda i: (jnp.maximum(i - half, 0), 0, 0)),
            pl.BlockSpec((d_model, TILE), lambda i: (0, i)),
        ],
        out_specs=[whole((rows // at, d_model)) for at in (2, 4, 8, 8)],
        out_shape=[shape_of((rows // 2, d_model), FULL)]
        + [shape_of((rows // at, d_model), LOW) for at in (4, 8, 8)],
        scratch_shapes=[pltpu.VMEM((rows, d_model), FULL)],
        compiler_params=params(58),
        cost_estimate=cost(7),
    )(gel_first, gel_rest, w_down)


def add_rows(out, rows):
    @pl.when(pl.program_id(0) == 0)
    def _():
        out[...] = jnp.zeros_like(out)

    for at, row in enumerate(rows):
        out[at : at + 1] += jnp.sum(row, axis=0, keepdims=True)


def turn_kernel(keep, got, last, resid, dy, gain, dh_out, dattn_out, sum_out):
    da2 = keep[...] + got[...].astype(FULL) + last[...].astype(FULL)
    unit, inverse = normalize(resid[...])
    dy_full = dy[...].astype(FULL)
    dh = dy_full + norm_back(da2, unit, inverse, gain[...].astype(FULL))
    dh_out[...] = dh
    dattn = dh.astype(LOW)
    dattn_out[...] = dattn
    add_rows(sum_out, (da2 * unit, da2, dattn.astype(FULL), dy_full))


def turn(keep, got, last, resid, dy, gain):
    dims = resid.shape
    block = pl.BlockSpec((BAND, dims[1]), lambda i: (i, 0))
    return pl.pallas_call(
        turn_kernel,
        grid=(dims[0] // BAND,),
        in_specs=[block] * 5 + [whole(gain.shape)],
        out_specs=[block, block, whole((4, dims[1]))],
        out_shape=[shape_of(dims, FULL), shape_of(dims, LOW), shape_of((4, dims[1]), FULL)],
        compiler_params=params(12),
        cost_estimate=cost(3),
    )(keep, got, last, resid, dy, gain)


def back_kernel(scale, own, near, far, last, w_out, qkv, probs_in, w_qkv, dqkv_out, sum_out, keep_out, send_out, fold_out, fold_last, act, total):
    step = pl.program_id(0)
    half = act.shape[0] // 2

    @pl.when(step == 0)
    def _():
        stack_rows(act, (own, near, far, last))
        total[...] = jnp.zeros_like(total)

    dmixed = dot(act[...], w_out[...], COLS).astype(LOW)
    for h in range(w_out.shape[1] // DH):
        at = slice(h * DH, (h + 1) * DH)
        probs = probs_in[h]
        dm = dmixed[:, at]
        dqkv_out[2, :, at] = dot(probs.astype(LOW), dm, ROWS).astype(LOW)
        dprobs = dot(dm, qkv[2, :, at], BOTH)
        terms = jnp.sum(probs * dprobs, axis=-1, keepdims=True)
        ds = (probs * (dprobs - terms) * scale).astype(LOW)
        dqkv_out[0, :, at] = dot(ds, qkv[1, :, at], COLS).astype(LOW)
        dqkv_out[1, :, at] = dot(ds, qkv[0, :, at], ROWS).astype(LOW)
    part = dot(dqkv_out[0], w_qkv[0], BOTH)
    part += dot(dqkv_out[1], w_qkv[1], BOTH)
    part += dot(dqkv_out[2], w_qkv[2], BOTH)
    total[...] += part
    for row, t in enumerate((0, 2)):
        sum_out[row : row + 1] = jnp.sum(dqkv_out[t].astype(FULL), axis=0, keepdims=True)

    @pl.when(step == pl.num_programs(0) - 1)
    def _():
        keep_out[...] = total[:half]
        send_out[...] = total[half : half + half // 2].astype(LOW)
        give_rows(total[half + half // 2 :].astype(LOW), (fold_out, fold_last))


def attention_back(own, near, far, last, w_out, qkv, probs, w_qkv, group=2):
    d_model, width = w_out.shape
    rows = qkv.shape[1]
    cols = group * DH
    return pl.pallas_call(
        functools.partial(back_kernel, DH**-0.5),
        grid=(width // cols,),
        in_specs=[
            *[whole(own.shape)] * 4,
            pl.BlockSpec((d_model, cols), lambda i: (0, i)),
            pl.BlockSpec((3, rows, cols), lambda i: (0, 0, i)),
            pl.BlockSpec((group, rows, rows), lambda i: (i, 0, 0)),
            pl.BlockSpec((3, d_model, cols), lambda i: (0, 0, i)),
        ],
        out_specs=[
            pl.BlockSpec((3, rows, cols), lambda i: (0, 0, i)),
            pl.BlockSpec((2, cols), lambda i: (0, i)),
            whole((rows // 2, d_model)),
            whole((rows // 4, d_model)),
            *[whole((rows // 8, d_model))] * 2,
        ],
        out_shape=[
            shape_of((3, rows, width), LOW),
            shape_of((2, width), FULL),
            shape_of((rows // 2, d_model), FULL),
            shape_of((rows // 4, d_model), LOW),
            *[shape_of((rows // 8, d_model), LOW)] * 2,
        ],
        scratch_shapes=[pltpu.VMEM((rows, d_model), LOW), pltpu.VMEM((rows, d_model), FULL)],
        compiler_params=params(48),
        cost_estimate=cost(15),
    )(own, near, far, last, w_out, qkv, probs, w_qkv)


def leave_kernel(keep, got, last, x_own, dh, gain, down_keep, down_got, down_last, resid, biases, *outs):
    da1 = keep[...] + got[...].astype(FULL) + last[...].astype(FULL)
    unit, inverse = normalize(x_own[...].astype(FULL))
    grad = (dh[...] + norm_back(da1, unit, inverse, gain[...].astype(FULL))).astype(LOW)
    down = down_keep[...] + down_got[...].astype(FULL) + down_last[...].astype(FULL)
    output = (resid[...] + down + biases[1:].astype(FULL)).astype(LOW)
    sub = output.shape[0]
    for at, out in enumerate(outs[:-1]):

        @pl.when(pl.program_id(0) == at)
        def _(out=out):
            out[:sub, :] = output
            out[sub:, :] = grad

    add_rows(outs[-1], (da1 * unit, da1))


def leave(keep, got, last, x_own, dh, gain, down_keep, down_got, down_last, resid, biases, parts):
    dims = x_own.shape
    rows = dims[0] // parts
    block = pl.BlockSpec((rows, dims[1]), lambda i: (i, 0))
    piece = (2 * rows, dims[1])
    return pl.pallas_call(
        leave_kernel,
        grid=(parts,),
        in_specs=[block] * 5 + [whole(gain.shape)] + [block] * 4 + [whole(biases.shape)],
        out_specs=[whole(piece)] * parts + [whole((2, dims[1]))],
        out_shape=[shape_of(piece, LOW)] * parts + [shape_of((2, dims[1]), FULL)],
        compiler_params=params(16),
        cost_estimate=cost(3),
    )(keep, got, last, x_own, dh, gain, down_keep, down_got, down_last, resid, biases)


def place_kernel(items, sub, spot, own, near, far, last, output, grad):
    for at, source in enumerate((own, near, far, last)):
        for s in range(items):
            row = 2 * s * sub
            output[spot[s], spot[items + at]] = source[row : row + sub, :]
            grad[spot[s], spot[items + at]] = source[row + sub : row + 2 * sub, :].astype(FULL)


def place(own, near, far, last, spot, items, mp):
    rows, d_model = own.shape
    sub = rows // items // 2
    vmem = pl.BlockSpec(memory_space=pltpu.VMEM)
    dims = (items, mp, sub, d_model)
    output, grad = pl.pallas_call(
        functools.partial(place_kernel, items, sub),
        in_specs=[pl.BlockSpec(memory_space=pltpu.SMEM)] + [vmem] * 4,
        out_specs=[vmem, vmem],
        out_shape=[shape_of(dims, LOW), shape_of(dims, FULL)],
        compiler_params=params(24),
        cost_estimate=cost(6),
    )(spot, own, near, far, last)
    return output.reshape(items, mp * sub, d_model), grad.reshape(items, mp * sub, d_model)


def product_kernel(counts, blocks, added, spots, *refs):
    out = refs[-1]
    refs = list(refs[:-1])
    columns = []
    for _ in range(blocks):
        columns.append([])
        for count in counts:
            pieces = [refs.pop(0)[...] for _ in range(count)]
            columns[-1].append(pieces[0] if count == 1 else jnp.concatenate(pieces, axis=0))
    units = [refs.pop(0) for _ in counts]
    for at in range(blocks):
        part = sum(dot(c, u[0], ROWS) for c, u in zip(columns[at], units))
        rows = part.shape[0]
        here = slice(at * rows, (at + 1) * rows)
        if added:
            part = part + refs[0][0, here].astype(FULL)
        out[0, here] = part.astype(LOW)


def products(spots, sources, blocks, chunk, added=None, block=0, start=0, count=None):
    if count is None:
        start, count = 0, sources[0][2].shape[0]
    in_specs, args = [], []
    for k in blocks:
        for pieces, base, _ in sources:
            for piece in pieces:
                at = k + base
                in_specs.append(pl.BlockSpec((piece.shape[0], chunk), lambda i, spots, at=at: (0, spots[at])))
                args.append(piece)
    for _, _, unit in sources:
        in_specs.append(pl.BlockSpec((1, unit.shape[1], TILE), lambda i, spots: (start + i, 0, 0)))
        args.append(unit)
    size = chunk * len(blocks)
    if added is not None:
        in_specs.append(pl.BlockSpec((1, size, TILE), lambda i, spots: (i, block, 0)))
        args.append(added)
    counts = tuple(len(pieces) for pieces, _, _ in sources)
    return pl.pallas_call(
        functools.partial(product_kernel, counts, len(blocks), added is not None),
        grid_spec=pltpu.PrefetchScalarGridSpec(
            num_scalar_prefetch=1,
            grid=(count,),
            in_specs=in_specs,
            out_specs=pl.BlockSpec((1, size, TILE), lambda i, spots: (i, 0, 0)),
        ),
        out_shape=shape_of((count, size, TILE), LOW),
        compiler_params=params(24),
        cost_estimate=cost(0.6 * count * len(blocks)),
    )(spots, *args)


def pass_kernel(got, mine, out):
    out[...] = (mine[...].astype(FULL) + got[...].astype(FULL)).astype(LOW)


def pass_on(got, mine, rows, start, count):
    steps = mine.shape[0]
    part = pl.BlockSpec((1, rows, TILE), lambda i, j: (i, start + j, 0))
    return pl.pallas_call(
        pass_kernel,
        grid=(steps, count),
        in_specs=[part, part],
        out_specs=pl.BlockSpec((1, rows, TILE), lambda i, j: (i, j, 0)),
        out_shape=shape_of((steps, count * rows, TILE), LOW),
        compiler_params=params(16),
        cost_estimate=cost(steps),
    )(got, mine)


def finish_kernel(n_inner, n_end, inner, *refs):
    out = refs[-1]
    for flag, terms in ((1, refs[:n_inner]), (0, refs[n_inner : n_inner + n_end])):

        @pl.when(inner[0] == flag)
        def _(terms=terms):
            out[...] = sum(term[...].astype(FULL) for term in terms).reshape(out.shape)


def finish(last, inner, inner_terms, end_terms, first, total, split, before):
    steps, chunk, _ = last.shape
    head = pl.BlockSpec((1, chunk, TILE), lambda i: (i, 0, 0))
    args = [inner, *inner_terms, *end_terms, last]
    in_specs = [pl.BlockSpec(memory_space=pltpu.SMEM)] + [head] * (len(args) - 1)
    aliases = {}
    if before is not None:
        aliases = {len(args): 0}
        in_specs.append(pl.BlockSpec(memory_space=pl.ANY))
        args.append(before)
    if split:
        out_spec = pl.BlockSpec((1, chunk, TILE), lambda i: (first + i, 0, 0))
        out_shape = shape_of((total, chunk, TILE), FULL)
    else:
        out_spec = pl.BlockSpec((chunk, TILE), lambda i: (0, first + i))
        out_shape = shape_of((chunk, total * TILE), FULL)
    return pl.pallas_call(
        functools.partial(finish_kernel, len(inner_terms), len(end_terms) + 1),
        grid=(steps,),
        in_specs=in_specs,
        out_specs=out_spec,
        out_shape=out_shape,
        input_output_aliases=aliases,
        compiler_params=params(16),
        cost_estimate=cost(steps),
    )(*args)


def join_kernel(*refs):
    stack_rows(refs[-1], refs[:-1])


def joined(first, *others):
    rows = first.shape[0] + sum(p.shape[0] for p in others)
    return pl.pallas_call(
        join_kernel,
        out_shape=shape_of((rows, first.shape[1]), LOW),
        compiler_params=params(16),
        cost_estimate=cost(1),
    )(first, *others)


class Names:
    def __getattr__(self, name):
        return name


N = Names()
PLAN = (
    (
        N.begin,
        (),
        ((N.y_act_one,), (N.c_act_one,)),
    ),
    (
        N.dy,
        (),
        ((N.d_act_one,), (N.y_dy, N.y_act_one), (N.c_dy,)),
    ),
    (
        N.attend,
        (),
        ((N.k_attn,), (N.l_attn,), (N.n_attn,), (N.x_mixed,), (N.d_dy,)),
    ),
    (
        N.fold_attn,
        (N.y_dy,),
        ((N.y_attn,), (N.e_dy,)),
    ),
    (
        N.norm_two,
        (N.x_mixed,),
        ((N.y_act_two,), (N.c_act_two,), (N.d_act_two,), (N.x_halves,)),
    ),
    (
        N.feed_one,
        (N.e_dy, N.n_attn, N.d_dy),
        ((N.x_u0,), (N.e_g0, N.e_dy), (N.y_halves,), (N.c_halves,)),
    ),
    (
        N.feed_two,
        (),
        ((N.k_da2,), (N.l_da2,), (N.n_da2,), (N.d_e_dy,)),
    ),
    (
        N.down,
        (N.d_act_two,),
        ((N.e_g1,), (N.k_down,), (N.l_down,), (N.n_down,)),
    ),
    (
        N.fold_da2,
        (N.y_halves, N.k_attn, N.x_halves),
        ((N.y_da2,), (N.d_halves,)),
    ),
    (
        N.cross_g0,
        (),
        ((N.m_g0,),),
    ),
    (
        N.norm_back_two,
        (),
        ((N.y_dattn,), (N.c_dattn,), (N.d_dattn,), (N.x_u1,)),
    ),
    (
        N.start_u0,
        (N.l_down,),
        (),
    ),
    (
        N.cross_g1,
        (),
        ((N.m_g1,), (N.e_u0,)),
    ),
    (
        N.attend_back,
        (N.x_u0,),
        ((N.k_da1,), (N.l_da1,), (N.n_da1,), (N.x_last, N.x_u1)),
    ),
    (
        N.start_u1,
        (),
        (),
    ),
    (
        N.fold_da1,
        (N.n_da1,),
        ((N.y_da1,), (N.x_q, N.x_last)),
    ),
    (
        N.fold_down,
        (),
        ((N.y_down, N.y_da1), (N.y_last, N.y_down)),
    ),
    (
        N.sum_up_g0,
        (),
        (),
    ),
    (
        N.cross_u0,
        (N.x_last,),
        ((N.m_u0, N.m_g1), (N.e_u1,)),
    ),
    (
        N.norm_back_one,
        (),
        ((N.c_last,), (N.d_last,)),
    ),
    (
        N.start_q0,
        (),
        ((N.x_g0,),),
    ),
    (
        N.start_o0,
        (),
        (),
    ),
    (
        N.start_q1,
        (N.k_da1,),
        (),
    ),
    (
        N.cross_u1,
        (N.e_u1,),
        ((N.e_o0,),),
    ),
    (
        N.sum_up_g1,
        (),
        ((N.x_g1,), (N.sum_tokens,)),
    ),
    (
        N.back_g0,
        (),
        ((N.o_g0,),),
    ),
    (
        N.cross_o0,
        (),
        ((N.e_q0,), (N.m_o0, N.m_u1), (N.m_u1, N.m_u0)),
    ),
    (
        N.back_u0,
        (),
        (),
    ),
    (
        N.back_g1,
        (),
        ((N.o_g1, N.o_u0), (N.o_u0, N.o_g0)),
    ),
    (
        N.end_u0,
        (),
        (),
    ),
    (
        N.back_u1,
        (),
        ((N.o_u1, N.o_g1),),
    ),
    (
        N.cross_q0,
        (),
        ((N.ends,), (N.m_q0, N.m_o0)),
    ),
    (
        N.end_g1,
        (),
        (),
    ),
    (
        N.ends_join,
        (),
        ((N.y_ends,), (N.c_ends,), (N.e_q1,)),
    ),
    (
        N.back_o0,
        (),
        ((N.o_o0, N.o_u1),),
    ),
    (
        N.end_u1,
        (),
        (),
    ),
    (
        N.end_o0,
        (),
        ((N.sum_dp,),),
    ),
    (
        N.end_g0,
        (),
        (),
    ),
    (
        N.cross_q1,
        (),
        ((N.m_q1,), (N.sum_one,), (N.d_ends,)),
    ),
    (
        N.back_q0,
        (),
        ((N.o_q0,),),
    ),
    (
        N.end_q0,
        (),
        (),
    ),
    (
        N.back_q1,
        (),
        ((N.o_q1,), (N.sum_two,)),
    ),
    (
        N.ends_place,
        (),
        (),
    ),
    (
        N.end_q1,
        (),
        (),
    ),
)
PLAIN = (
    N.begin,
    N.dy,
    N.attend,
    N.fold_attn,
    N.norm_two,
    N.feed_one,
    N.feed_two,
    N.down,
    N.fold_da2,
    N.norm_back_two,
    N.attend_back,
    N.fold_da1,
    N.fold_down,
    N.norm_back_one,
    N.ends_join,
    N.ends_place,
)
PLAIN_SENDS = (
    N.y_act_one,
    N.c_act_one,
    N.d_act_one,
    N.y_dy,
    N.c_dy,
    N.k_attn,
    N.l_attn,
    N.n_attn,
    N.d_dy,
    N.y_attn,
    N.y_act_two,
    N.c_act_two,
    N.d_act_two,
    N.k_da2,
    N.l_da2,
    N.n_da2,
    N.k_down,
    N.l_down,
    N.n_down,
    N.y_da2,
    N.y_dattn,
    N.c_dattn,
    N.d_dattn,
    N.k_da1,
    N.l_da1,
    N.n_da1,
    N.y_da1,
    N.y_down,
    N.sum_tokens,
    N.ends,
    N.y_ends,
    N.c_ends,
    N.sum_dp,
    N.sum_one,
    N.d_ends,
    N.sum_two,
)


def on_device(
    dp,
    blk,
    mp,
    inputs,
    lengths,
    w_qkv,
    b_qv,
    w_out,
    out_biases,
    ln_gains,
    ln_shifts,
    w_up,
    b_up,
    w_down,
    cotangent,
):
    items, block_len, d_model = inputs.shape
    width = w_qkv.shape[2]
    sub = block_len // mp
    own_rows = blk * sub
    rows = own_rows * mp
    chunk = d_model // (dp * blk)
    half_cols = blk * chunk
    paired = dp == 2
    order = Order()
    x, z, me = lax.axis_index("dp"), lax.axis_index("blk"), lax.axis_index("mp")

    def swap_core(array):
        return lax.ppermute(array, "mp", flip(mp, 1))

    def swap_y(array):
        return lax.ppermute(array, "mp", flip(mp, 2))

    def swap_dp(array):
        return lax.ppermute(array, "dp", flip(dp, 1))

    def along(array, pairs):
        return lax.ppermute(array, "blk", pairs)

    def to_items(array, *ties):
        mine = lax.dynamic_slice_in_dim(array, me * sub, sub, axis=1)
        parts = {0: lax.dynamic_index_in_dim(mine, z, 0, keepdims=False)}
        for s in (1, blk - 1, 2):
            piece = lax.dynamic_index_in_dim(mine, lax.rem(z + s, blk), 0, keepdims=False)
            if ties:
                piece = after(piece, *ties)
            parts[s] = along(piece, shift(blk, s))
        return [parts[s] for s in range(blk)]

    spot = jnp.stack(
        [lax.rem(z + s, blk) for s in range(blk)] + [me ^ j for j in (0, 2, 1, 3)]
    ).astype(jnp.int32)
    in_block = jnp.arange(sub, dtype=jnp.int32)
    block_of = lax.rem(z - jnp.arange(blk, dtype=jnp.int32) + blk, blk)

    def positions_of(q):
        return (block_of[:, None] * block_len + q * sub + in_block[None, :]).reshape(-1)

    pos = jnp.concatenate([positions_of(me ^ j) for j in (0, 2, 1, 3)])
    length = lax.dynamic_slice_in_dim(lengths, z, 1)

    def other_half(array):
        return lax.dynamic_slice_in_dim(array, (1 - x) * half_cols, half_cols, axis=1)

    line = [jnp.where(z < blk // 2, k, blk - 1 - k) for k in range(blk)]
    inner = jnp.where((z == 0) | (z == blk - 1), 0, 1).astype(jnp.int32)[None]
    MINE, HALF, SECOND, THEIRS = (blk * i for i in range(4))
    spots = jnp.stack(
        [x * blk + at for at in line]
        + line
        + [blk + at for at in line]
        + [(1 - x) * blk + at for at in line]
    ).astype(jnp.int32)
    to_inner, across, to_end = [(0, 1), (3, 2)], [(1, 2), (2, 1)], [(1, 0), (2, 3)]

    def grad_plain(full, unit):
        part = jnp.einsum("rd,trc->dtc", jnp.concatenate(full), unit, preferred_element_type=FULL)
        part = lax.psum_scatter(part.astype(LOW), ("dp", "blk"), scatter_dimension=0, tiled=True)
        return part.astype(FULL)

    w_three = w_qkv.transpose(1, 0, 2)
    b_three = jnp.stack([b_qv[0], jnp.zeros_like(b_qv[0]), b_qv[1]]).astype(FULL)
    gain_one, gain_two = ln_gains[:1], ln_gains[1:]
    shift_one, shift_two = ln_shifts[:1], ln_shifts[1:]
    tiles = w_up.shape[1] // TILE
    some = tiles // 2
    b_row = b_up[None]
    v = {}
    steps = {}
    sends = {}

    def step(function):
        steps[function.__name__] = function
        return function

    def send(name, swap, *operand):
        def run(needs):
            value = operand[0]() if callable(operand[0]) else v[operand[0]]
            ties = [v[need] for need in (*operand[1:], *needs)]
            v[name] = swap(after(value, order.last, *jax.tree.leaves(ties)))

        sends[name] = run

    def cut(array, parts):
        rows = array.shape[0] // parts
        return [array[i * rows : (i + 1) * rows] for i in range(parts)]

    def gather(name, own):
        send(N.y_ + name, swap_y, own)
        send(N.c_ + name, swap_core, own)
        send(N.d_ + name, swap_core, N.y_ + name)

    def gathered(name, own):
        return [v[own], v[N.y_ + name], v[N.c_ + name], v[N.d_ + name]]

    def scatter(name):
        send(N.k_ + name, swap_core, N.t_ + name)
        send(N.l_ + name, swap_core, N.u_ + name)
        send(N.n_ + name, swap_core, N.w_ + name)
        send(N.y_ + name, swap_y, N.f_ + name)

        def fold_it():
            v[N.f_ + name] = order.run(
                fold, v[N.l_ + name], v[N.n_ + name], v[N.keep_ + name]
            )

        steps[N.fold_ + name] = fold_it

    def scattered(name):
        return [v[N.keep_ + name], v[N.k_ + name], v[N.y_ + name]]

    def terms_of(name, terms):
        v[N.keep_ + name], v[N.t_ + name], v[N.u_ + name], v[N.w_ + name] = terms

    x_parts = to_items(inputs)
    dy_parts = to_items(cotangent, *x_parts[1:])
    gather(N.act_one, N.act_one_own)
    gather(N.dy, N.dy_own)
    gather(N.act_two, N.act_two_own)
    gather(N.dattn, N.dattn_own)
    for name in (N.attn, N.da2, N.down, N.da1):
        scatter(name)

    @step
    def begin():
        v[N.x_own], v[N.act_one_own] = enter(x_parts[0], gain_one, shift_one, *x_parts[1:])
        order.last = v[N.act_one_own]

    @step
    def dy():
        v[N.dy_own] = order.run(masked, dy_parts[0], length, pos[:own_rows, None], *dy_parts[1:])

    @step
    def attend():
        own, *others = gathered(N.act_one, N.act_one_own)
        v[N.qkv], v[N.probs], v[N.mixed], *terms = order.run(
            attention, own, *others, w_three, b_three, w_out, pos, length
        )
        terms_of(N.attn, terms)

    send(N.x_mixed, swap_dp, N.mixed)
    send(
        N.e_dy,
        lambda array: along(array, to_inner),
        lambda: jnp.concatenate([v[N.dy_own], v[N.y_dy]], axis=0),
    )
    send(N.d_e_dy, swap_core, N.e_dy)

    @step
    def norm_two():
        keep, got, last = scattered(N.attn)
        v[N.resid], v[N.act_two_own] = order.run(
            middle, v[N.x_own], keep, got, last, out_biases, gain_two, shift_two
        )

    send(
        N.x_halves,
        swap_dp,
        lambda: jnp.concatenate(
            [other_half(v[name]) for name in (N.act_one_own, N.act_two_own)], axis=1
        ),
    )
    gather(N.halves, N.x_halves)

    def feed_half(before, first):
        own, *others = gathered(N.act_two, N.act_two_own)
        dy = gathered(N.dy, N.dy_own)
        return order.run(feed, own, *others, dy, w_up, b_row, w_down, before, first, some)

    @step
    def feed_one():
        v[N.gel_a], v[N.dup_a], v[N.up_sum_a], v[N.before] = feed_half(None, 0)

    @step
    def feed_two():
        v[N.gel_b], v[N.dup_b], v[N.up_sum_b], *terms = feed_half(v[N.before], some)
        terms_of(N.da2, terms)

    send(N.x_u0, swap_dp, N.dup_a)
    send(N.x_u1, swap_dp, N.dup_b)

    @step
    def down():
        terms_of(N.down, order.run(down_part, v[N.gel_a], v[N.gel_b], w_down))

    @step
    def norm_back_two():
        keep, got, last = scattered(N.da2)
        v[N.dh], v[N.dattn_own], v[N.sums_two] = order.run(
            turn, keep, got, last, v[N.resid], v[N.dy_own], gain_two
        )

    send(N.x_last, swap_dp, lambda: other_half(v[N.dattn_own]))
    gather(N.last, N.x_last)

    @step
    def attend_back():
        own, *others = gathered(N.dattn, N.dattn_own)
        v[N.dqkv], v[N.qkv_sum], *terms = order.run(
            attention_back, own, *others, w_out, v[N.qkv], v[N.probs], w_three
        )
        terms_of(N.da1, terms)

    send(N.x_q, swap_dp, N.dqkv)

    @step
    def norm_back_one():
        *v[N.ends_parts], v[N.sums_one] = order.run(
            leave,
            *scattered(N.da1),
            v[N.x_own],
            v[N.dh],
            gain_one,
            *scattered(N.down),
            v[N.resid],
            out_biases,
            blk,
        )

    def move_ends(parts):
        return [parts[0]] + [along(parts[s], shift(blk, -s)) for s in range(1, blk)]

    def ends(needs):
        tie = [order.last, *[v[n] for n in needs]]
        v[N.ends] = move_ends([after(part, *tie) for part in v[N.ends_parts]])

    sends[N.ends] = ends

    def sum_tokens(needs):
        tie = [order.last, *[v[n] for n in needs]]
        sums = jnp.concatenate([v[N.sums_one], v[N.sums_two]], axis=0).reshape(-1)
        sums = after(sums, *tie)
        sums = sums + swap_core(sums)
        sums = sums + swap_y(sums)
        rest = [v[name].reshape(-1) for name in (N.qkv_sum, N.up_sum_a, N.up_sum_b)]
        v[N.sums] = jnp.concatenate([sums, *rest])

    def sum_dp(needs):
        sums = after(v[N.sums], order.last, *[v[n] for n in needs])
        bit = 1
        while bit < dp:
            sums = sums + lax.ppermute(sums, "dp", flip(dp, bit))
            bit *= 2
        v[N.sums] = sums

    def sum_step(bit):
        def run(needs):
            sums = after(v[N.sums], order.last, *[v[n] for n in needs])
            v[N.sums] = sums + along(sums, flip(blk, bit))

        return run

    sends[N.sum_tokens] = sum_tokens
    sends[N.sum_one] = sum_step(1)
    sends[N.sum_two] = sum_step(2)
    sends[N.sum_dp] = sum_dp

    @step
    def ends_join():
        v[N.ends_own] = order.run(joined, *v[N.ends])

    gather(N.ends, N.ends_own)

    @step
    def ends_place():
        v[N.output], v[N.input_grad] = order.run(
            place, *gathered(N.ends, N.ends_own), spot, items, mp
        )

    def token_piece(name, first, unit):
        def sources():
            ends = [v[N.e_dy], v[N.d_e_dy]]
            return [(gathered(N.dy, N.dy_own), MINE, v[unit]), (ends, MINE, v[N.e_ + name])]

        def cross():
            blocks = (2, 3, 2 + THEIRS, 3 + THEIRS)
            v[N.cross_ + name] = order.run(products, spots, sources(), blocks, chunk)

        def sum_up():
            blocks = (1, 0, 1 + THEIRS, THEIRS)
            v[N.all_ + name] = order.run(
                products, spots, sources(), blocks, chunk, v[N.m_ + name]
            )

        def back():
            v[N.back_ + name] = order.run(
                pass_on, v[N.x_ + name], v[N.all_ + name], chunk, 1, 1
            )

        def end():
            terms = [v[N.all_ + name], v[N.x_ + name]]
            v[N.grad_down] = order.run(
                finish, v[N.o_ + name], inner, terms, [], first, tiles, False, v.get(N.grad_down)
            )

        for function in (cross, sum_up, back, end):
            steps[function.__name__ + N._ + name] = function
        send(N.e_ + name, lambda array: along(array, to_inner), unit)
        send(N.m_ + name, lambda array: along(array, across), N.cross_ + name)
        send(N.x_ + name, swap_dp, lambda: v[N.all_ + name][:, 2 * chunk :])
        send(N.o_ + name, lambda array: along(array, to_end), N.back_ + name)

    def sum_piece(name, columns, units, target, first, total, split, count=None):
        def sources():
            return [(c(), base, u) for (c, base), u in zip(columns, units())]

        def start():
            v[N.mine_ + name] = order.run(
                products, spots, sources(), (1, 2, 3), chunk, None, 0, first, count
            )

        def cross():
            v[N.cross_ + name] = order.run(
                pass_on, v[N.e_ + name], v[N.mine_ + name], chunk, 1, 2
            )

        def back():
            v[N.back_ + name] = order.run(
                products, spots, sources(), (0,), chunk, v[N.m_ + name], 1, first, count
            )

        def end():
            terms = [v[N.mine_ + name], v[N.e_ + name], v[N.m_ + name]]
            v[target] = order.run(
                finish, v[N.o_ + name], inner, terms, [v[N.back_ + name]], first, total, split, v.get(target)
            )

        for function in (start, cross, back, end):
            steps[function.__name__ + N._ + name] = function
        send(N.e_ + name, lambda array: along(array, to_inner), N.mine_ + name)
        send(N.m_ + name, lambda array: along(array, across), N.cross_ + name)
        send(N.o_ + name, lambda array: along(array, to_end), N.back_ + name)

    def columns_of(name, own):
        return lambda: gathered(name, own)

    act_one, act_two, dattn, halves, last = (
        columns_of(name, own)
        for name, own in (
            (N.act_one, N.act_one_own),
            (N.act_two, N.act_two_own),
            (N.dattn, N.dattn_own),
            (N.halves, N.x_halves),
            (N.last, N.x_last),
        )
    )
    token_piece(N.g0, 0, N.gel_a)
    token_piece(N.g1, some, N.gel_b)
    both = [(act_two, MINE), (halves, SECOND)]
    sum_piece(N.u0, both, lambda: [v[N.dup_a], v[N.x_u0]], N.grad_up, 0, tiles, False)
    sum_piece(N.u1, both, lambda: [v[N.dup_b], v[N.x_u1]], N.grad_up, some, tiles, False)
    both = [(act_one, MINE), (halves, HALF)]
    sum_piece(N.q0, both, lambda: [v[N.dqkv], v[N.x_q]], N.grad_qkv, 0, 3, True, 2)
    sum_piece(N.q1, both, lambda: [v[N.dqkv], v[N.x_q]], N.grad_qkv, 2, 3, True, 1)
    both = [(dattn, MINE), (last, HALF)]
    sum_piece(N.o0, both, lambda: [v[N.mixed][None], v[N.x_mixed][None]], N.grad_out, 0, 1, False)

    for name, needs, starts in PLAN:
        if paired or name in PLAIN:
            order.needs = [leaf for need in needs if need in v for leaf in jax.tree.leaves(v[need])]
            with jax.named_scope(name):
                steps[name]()
        for entry in starts:
            transfer, *ties = entry
            if paired or transfer in PLAIN_SENDS:
                with jax.named_scope(transfer):
                    sends[transfer]([tie for tie in ties if tie in v])
    if paired:
        grad_qkv = v[N.grad_qkv].transpose(1, 0, 2)
    else:
        gel = jnp.concatenate([v[N.gel_a], v[N.gel_b]], axis=0)
        dup = jnp.concatenate([v[N.dup_a], v[N.dup_b]], axis=0)
        v[N.grad_down] = grad_plain(gathered(N.dy, N.dy_own), gel).reshape(chunk, -1)
        v[N.grad_up] = grad_plain(act_two(), dup).reshape(chunk, -1)
        v[N.grad_out] = grad_plain(dattn(), v[N.mixed][None]).reshape(chunk, -1)
        grad_qkv = grad_plain(act_one(), v[N.dqkv])

    sums = v[N.sums]
    per_token = sums[: 6 * d_model].reshape(6, d_model)
    grad_qv_bias = sums[6 * d_model : 6 * d_model + 2 * width].reshape(2, width)
    return (
        v[N.output],
        v[N.input_grad],
        grad_qkv,
        grad_qv_bias,
        v[N.grad_out],
        per_token[4:6],
        jnp.stack([per_token[0], per_token[2]]),
        jnp.stack([per_token[1], per_token[3]]),
        v[N.grad_up],
        sums[6 * d_model + 2 * width :],
        v[N.grad_down],
    )


def solution(mesh):
    sizes = [mesh.shape[name] for name in ("dp", "blk", "mp")]
    in_specs = (
        P("dp", "blk", None),
        P("dp"),
        P(None, None, "mp"),
        P(None, "mp"),
        P(None, "mp"),
        P(),
        P(),
        P(),
        P(None, "mp"),
        P("mp"),
        P(None, "mp"),
        P("dp", "blk", None),
    )
    out_specs = (
        P("dp", "blk", None),
        P("dp", "blk", None),
        P(("dp", "blk"), None, "mp"),
        P(None, "mp"),
        P(("dp", "blk"), "mp"),
        P(),
        P(),
        P(),
        P(("dp", "blk"), "mp"),
        P("mp"),
        P(("dp", "blk"), "mp"),
    )

    def step(*arrays):
        return on_device(*sizes, *arrays)

    return jax.shard_map(
        step, mesh=mesh, in_specs=in_specs, out_specs=out_specs, check_vma=False
    )
```
